128 devices in a mesh: clip: 4 (over y_hi, core), tile: 32 (over y_lo, x, z).
Axes of the slice: x: 4, y: 4 (y_hi: 2, y_lo: 2; y = y_hi * 2 + y_lo), z: 4, core: 2. Of those that a mesh axis runs over, the one named last changes fastest.
Arguments:
- features: bfloat16 [8, 16, 64, 12, 384], P('clip', None, 'tile'), may hold values from -6 to 6
- pixel_grad: bfloat16 [8, 16, 64, 12, 384], P('clip', None, 'tile'), may hold values from -6 to 6
- frame_list: int32 [8, 16], P('clip'), may hold values from -1 to 15, as said below
- conv_weight: bfloat16 [3, 3, 3, 384, 384], replicated, may hold values from -0.0625 to 0.0625
- in_weight: bfloat16 [3, 3, 3, 16, 384], replicated, may hold values from -0.3125 to 0.3125
- last_hidden: bfloat16 [24576, 5120], P(('clip', 'tile')), may hold values from -6 to 6
- modulation: float32 [8, 2, 5120], P('clip'), may hold values from -3 to 3
- head_weight: bfloat16 [5120, 64], replicated, may hold values from -0.75 to 0.75
Outputs:
- hidden_grad: bfloat16 [24576, 5120], P(('clip', 'tile'))
- head_weight_grad: float32 [5120, 64], replicated
- modulation_grad: float32 [8, 2, 5120], P('clip')
- conv_weight_grad: float32 [3, 3, 3, 384, 384], P(None, None, None, 'tile')
The draws below stay inside these ranges and needn't reach their ends.
Inputs may be any that keep to these rules, and one draw needn't show every extreme that they name: `frame_list`: each clip's list holds between 2 and 16 distinct frame numbers first, then -1; some clip lists every frame.
All inputs are finite; a program needn't handle non-finite values.
Results may differ from the reference program's by a relative error of at most 0.006.
Values may be sent and summed in bfloat16 or wider, within the bound.
No kernel may reach another device: no remote copies, remote signals or barrier semaphores. Data moves between devices by JAX's collectives and lax.ppermute only.
A program may use at most 192 MiB of HBM per device.

```python
import jax
import jax.numpy as jnp
from jax import lax

D = 5120
Z = 16
CIN = 384
COUT = 384
FRAMES = 16
COLS = 12
CLIPS = 8
ROWS = 64
TOKROWS = 32
TOKCOLS = 6
TOKENS = 24576
OUTF = 64


def draw_frame_list(key, part):
    key = jax.random.fold_in(key, 7)
    order_key, count_key, full_key = jax.random.split(key, 3)
    orders = jax.vmap(lambda subkey: jax.random.permutation(subkey, FRAMES))(jax.random.split(order_key, CLIPS))
    counts = jax.random.randint(count_key, (CLIPS,), 2, FRAMES + 1)
    fullest = jax.random.randint(full_key, (), 0, CLIPS)
    counts = jnp.where(jnp.arange(CLIPS) == fullest, FRAMES, counts)
    listed = jnp.where(jnp.arange(FRAMES)[None, :] < counts[:, None], orders, -1)
    return listed.astype(jnp.int32)


def block_levels(stream_key, shape, pieces, least, top_value):
    level, own = 1.0, jax.random.fold_in(stream_key, 6)
    for axis_at, shards_of in pieces:
        steps = jnp.exp(jax.random.uniform(jax.random.fold_in(own, axis_at), (shards_of,), jnp.float32, least / len(pieces), top_value / len(pieces)))
        level = level * jnp.repeat(steps, shape[axis_at] // shards_of).reshape([-1 if axis == axis_at else 1 for axis in range(len(shape))])
    return level


def bell_draw(rng, dims, deviation, most, shards=(), held_as=jnp.bfloat16):
    values = deviation * jax.random.normal(rng, dims, jnp.float32)
    if shards:
        values = values * block_levels(rng, dims, shards, -0.22, 0.18)
    return jnp.clip(values, -most, most).astype(held_as)


def setup_inputs(seed: int = 0) -> dict:
    splits = jax.random.split(jax.random.key(seed), 9)
    return {
        "features": bell_draw(splits[0], (CLIPS, FRAMES, ROWS, COLS, CIN), 1.0, 6.0, ((0, 4), (2, 32))),
        "pixel_grad": bell_draw(splits[1], (CLIPS, FRAMES, ROWS, COLS, COUT), 1.0, 6.0, ((0, 4), (2, 32))),
        "frame_list": draw_frame_list(jax.random.fold_in(splits[8], 71), 0),
        "conv_weight": bell_draw(splits[3], (3, 3, 3, CIN, COUT), (27 * CIN) ** -0.5, 0.0625),
        "in_weight": bell_draw(splits[4], (3, 3, 3, Z, CIN), (27 * Z) ** -0.5, 0.3125),
        "last_hidden": bell_draw(splits[5], (TOKENS, D), 1.0, 6.0, ((0, 128),)),
        "modulation": bell_draw(splits[6], (CLIPS, 2, D), 0.5, 3.0, ((0, 4),), jnp.float32),
        "head_weight": bell_draw(splits[7], (D, OUTF), OUTF ** -0.5, 0.75),
    }


def silu_slope(values):
    sig = jax.nn.sigmoid(values)
    return sig * (1.0 + values * (1.0 - sig))

def shifted(padded_grad, out_rows, row_taps):
    frames = padded_grad.shape[1]
    columns = padded_grad.shape[3]
    widened = jnp.pad(padded_grad, ((0, 0), (0, 2), (0, 0), (1, 1), (0, 0)))
    windows = []
    for time_tap in range(3):
        for row_tap in row_taps:
            for col_tap in (-1, 0, 1):
                window = widened[:, time_tap:time_tap + frames, 1 - row_tap:1 - row_tap + out_rows, 1 - col_tap:1 - col_tap + columns, :]
                windows.append(((time_tap, row_tap + 1, col_tap + 1), window))
    return windows

def conv_back(padded_grad, weight, out_rows, row_taps):
    summed = None
    shape = None
    for (time_tap, row_tap, col_tap), window in shifted(padded_grad, out_rows, row_taps):
        shape = window.shape[:-1] + (weight.shape[3],)
        product = jnp.dot(window.reshape(-1, window.shape[-1]), weight[time_tap, row_tap, col_tap].T, preferred_element_type=jnp.float32)
        summed = product if summed is None else summed + product
    return summed.reshape(shape)

def weight_grad(activations, padded_grad, out_rows):
    flattened = activations.reshape(-1, activations.shape[-1])
    gradients = [jnp.dot(flattened.T, window.reshape(-1, window.shape[-1]), preferred_element_type=jnp.float32) for _, window in shifted(padded_grad, out_rows, (-1, 0, 1))]
    return jnp.stack(gradients).reshape(3, 3, 3, flattened.shape[1], padded_grad.shape[-1])

def pad_rows(values):
    return jnp.pad(values, ((0, 0), (0, 0), (1, 1), (0, 0), (0, 0)))

def reference(features, pixel_grad, frame_list, conv_weight, in_weight, last_hidden, modulation, head_weight):
    scored = jnp.any(frame_list[:, None, :] == jnp.arange(FRAMES, dtype=jnp.int32)[None, :, None], axis=-1)
    masked = pixel_grad * scored.astype(jnp.bfloat16)[:, :, None, None, None]

    def decode_clip(pair):
        feats, grads = pair
        feats = feats[None]
        grads = grads[None]
        activation = jax.nn.silu(feats.astype(jnp.float32)).astype(jnp.bfloat16)
        padded = pad_rows(grads)
        grad_act = conv_back(padded, conv_weight, ROWS, (-1, 0, 1))
        partial_w = weight_grad(activation, padded, ROWS)
        grad_feat = (grad_act * silu_slope(feats.astype(jnp.float32))).astype(jnp.bfloat16)
        latent = conv_back(pad_rows(grad_feat), in_weight, ROWS, (-1, 0, 1)).astype(jnp.bfloat16)
        return (latent[0], partial_w)
    latent_grad, partials = lax.map(decode_clip, (features, masked))
    conv_weight_grad = lax.optimization_barrier(jnp.sum(partials, axis=0))
    patches = latent_grad.reshape(CLIPS, FRAMES, TOKROWS, 2, TOKCOLS, 2, Z)
    patches = jnp.transpose(patches, (0, 1, 2, 4, 3, 5, 6)).reshape(CLIPS, FRAMES * TOKROWS * TOKCOLS, OUTF)
    hidden = last_hidden.reshape(CLIPS, FRAMES * TOKROWS * TOKCOLS, D)

    def head_clip(triple):
        states, patch_grad, mods = triple
        states = states.astype(jnp.float32)
        average = lax.optimization_barrier(jnp.mean(states, axis=-1, keepdims=True))
        centered = states - average
        inv_std = lax.rsqrt(lax.optimization_barrier(jnp.mean(centered * centered, axis=-1, keepdims=True)) + 1e-06)
        normed = centered * inv_std
        head_input = (normed * (1.0 + mods[1]) + mods[0]).astype(jnp.bfloat16)
        w_grad = jnp.dot(head_input.T, patch_grad, preferred_element_type=jnp.float32)
        grad_input = jnp.dot(patch_grad, head_weight.T, preferred_element_type=jnp.float32)
        mod_grad = jnp.stack([lax.optimization_barrier(jnp.sum(grad_input, axis=0)), lax.optimization_barrier(jnp.sum(grad_input * normed, axis=0))])
        scaled = grad_input * (1.0 + mods[1])
        result = (scaled - lax.optimization_barrier(jnp.mean(scaled, axis=-1, keepdims=True)) - normed * lax.optimization_barrier(jnp.mean(scaled * normed, axis=-1, keepdims=True))) * inv_std
        return (result.astype(jnp.bfloat16), w_grad, mod_grad)
    hidden_grad, w_grads, modulation_grad = lax.map(head_clip, (hidden, patches, modulation))
    return (hidden_grad.reshape(TOKENS, D), lax.optimization_barrier(jnp.sum(w_grads, axis=0)), modulation_grad, conv_weight_grad)
```

```python
import functools

import jax
import jax.numpy as jnp
from jax import lax
from jax.experimental import pallas as pl
from jax.experimental.pallas import tpu as pltpu
from jax.sharding import PartitionSpec as P

F32 = jnp.float32
BF16 = jnp.bfloat16
BOTH = ("clip", "tile")
FRAMES = 16
SPAN = 32
COLS = 12
CH = 384
WIDTH = 5120
HALF = 2560
STEP = 512
PIECE = 384
LOAD = HALF + PIECE
BACK = HALF + 2 * PIECE
TAPS = 14
VMEM = 56 * 1024 * 1024


def place(clip, tile):
    return (clip // 2) * 2 + tile // 16, (tile // 4) % 4, tile % 4, clip % 2


def number(y, x, z, core):
    return ((y // 2) * 2 + core) * 32 + (y % 2) * 16 + x * 4 + z


def pairs(shift_of):
    out = []
    for source in range(128):
        where = place(source // 32, source % 32)
        out.append((source, number(*shift_of(*where))))
    return out


def along(core_axis, steps):
    def shift(y, x, z, core):
        if core == core_axis:
            return y, x, (z + steps) % 4, core
        return y, (x + steps) % 4, z, core

    return pairs(shift)


def along_y(steps):
    return pairs(lambda y, x, z, core: ((y + steps) % 4, x, z, core))


OTHER_CORE = pairs(lambda y, x, z, core: (y, x, z, 1 - core))


def shift_frames(tile, steps):
    if steps == 0:
        return tile
    count = tile.shape[0]
    moved = pltpu.roll(tile, count - steps, 0)
    frame = lax.broadcasted_iota(jnp.int32, tile.shape, 0) & (FRAMES - 1)
    return jnp.where(frame < FRAMES - steps, moved, 0.0)


def fill_windows(windows, rows, base):
    blank = jnp.zeros((SPAN, CH), BF16)
    for row, source in enumerate(rows):
        for time_tap in range(3):
            windows[time_tap, row, 0, pl.ds(base, SPAN)] = blank
            windows[time_tap, row, COLS + 1, pl.ds(base, SPAN)] = blank

        def column(col, carry, row=row, source=source):
            tile = source[col]
            windows[0, row, col + 1, pl.ds(base, SPAN)] = tile
            wide = tile.astype(F32)
            for time_tap in (1, 2):
                windows[time_tap, row, col + 1, pl.ds(base, SPAN)] = shift_frames(
                    wide, time_tap
                ).astype(BF16)
            return carry

        lax.fori_loop(0, COLS, column, 0)


def lanes_dot(left, right):
    return lax.dot_general(left, right, (((1,), (1,)), ((), ())), preferred_element_type=F32)


def grad_kernel(own, low, high, feats, weight, in_weight, out, windows, total, grads, spread):
    step = pl.program_id(0)

    @pl.when(step == 0)
    def _():
        fill_windows(windows, (low, own.at[0], own.at[1], high), 0)
        blank = jnp.zeros((16, CH), BF16)
        for time_tap in range(3):
            for rowout in range(4):
                for parity in range(2):
                    at = ((time_tap * 4 + rowout) * 2 + parity) * 16
                    for near in range(4):
                        for side in range(2):
                            row_tap = rowout - side
                            col_tap = parity + 2 - near
                            inside = 0 <= row_tap <= 2 and 0 <= col_tap <= 2
                            value = in_weight[time_tap, row_tap, col_tap] if inside else blank
                            spread[at : at + 16, pl.ds((near * 2 + side) * CH, CH)] = value

    for row_tap in range(3):
        left = jnp.concatenate(
            [
                windows[step, pl.ds(2 - row_tap, 2), pl.ds(2 - col_tap, COLS)].reshape(-1, CH)
                for col_tap in range(3)
            ],
            axis=1,
        )
        right = jnp.concatenate([weight[0, row_tap, col_tap] for col_tap in range(3)], axis=1)
        product = lanes_dot(left, right)
        if row_tap == 0:

            @pl.when(step == 0)
            def _():
                total[...] = product

            @pl.when(step != 0)
            def _():
                total[...] += product
        else:
            total[...] += product

    @pl.when(step == 2)
    def _():
        blank = jnp.zeros((SPAN, CH), BF16)
        for side in range(2):
            grads[side, 0, 0] = blank
            grads[side, 6, 1] = blank
            for col in range(COLS):
                values = feats[side, col].astype(F32)
                sig = jax.nn.sigmoid(values)
                slope = sig * (1.0 + values * (1.0 - sig))
                product = total[pl.ds((side * COLS + col) * SPAN, SPAN)] * slope
                grads[side, (col + 1) // 2, (col + 1) % 2] = product.astype(BF16)
        left = jnp.concatenate(
            [
                grads[side, pl.ds(near // 2, 6), near % 2].reshape(-1, CH)
                for near in range(4)
                for side in range(2)
            ],
            axis=1,
        )
        latent = lanes_dot(left, spread[...])
        for pair in range(6):
            block = latent[pair * SPAN : (pair + 1) * SPAN]
            out[:, pair * 128 : (pair + 1) * 128] = (
                block[:, 0:128]
                + shift_frames(block[:, 128:256], 1)
                + shift_frames(block[:, 256:384], 2)
            )


def input_grad(own, low, high, feats, conv_weight, in_weight):
    whole = lambda shape: pl.BlockSpec(shape, lambda i: (0,) * len(shape))
    return pl.pallas_call(
        grad_kernel,
        grid=(3,),
        in_specs=[
            whole((2, COLS, SPAN, CH)),
            whole((COLS, SPAN, CH)),
            whole((COLS, SPAN, CH)),
            whole((2, COLS, SPAN, CH)),
            pl.BlockSpec((1, 3, 3, CH, CH), lambda i: (i, 0, 0, 0, 0)),
            whole((3, 3, 3, 16, CH)),
        ],
        out_specs=whole((SPAN, 768)),
        out_shape=jax.ShapeDtypeStruct((SPAN, 768), F32),
        scratch_shapes=[
            pltpu.VMEM((3, 4, COLS + 2, SPAN, CH), BF16),
            pltpu.VMEM((2 * COLS * SPAN, CH), F32),
            pltpu.VMEM((2, 7, 2, SPAN, CH), BF16),
            pltpu.VMEM((384, 8 * CH), BF16),
        ],
        compiler_params=pltpu.CompilerParams(vmem_limit_bytes=VMEM),
        cost_estimate=pl.CostEstimate(
            flops=2 * 768 * 27 * CH * CH, bytes_accessed=12_000_000, transcendentals=768 * CH
        ),
        name="input_grad",
    )(own, low, high, feats, conv_weight, in_weight)


def weight_kernel(
    core, own, low, high, feats, own2, low2, high2, feats2, order,
    out0, out1, out2, out3, windows, active, turned,
):
    step = pl.program_id(0)

    @pl.when(step == 0)
    def _():
        fill_windows(windows, (low, own.at[0], own.at[1], high), 0)
        fill_windows(windows, (low2, own2.at[0], own2.at[1], high2), SPAN)
        for base, source in ((0, feats), (SPAN, feats2)):
            for side in range(2):

                def column(col, carry, base=base, source=source, side=side):
                    values = source[side, col].astype(F32)
                    active[side, col, pl.ds(base, SPAN)] = jax.nn.silu(values).astype(BF16)
                    return carry

                lax.fori_loop(0, COLS, column, 0)
        turned[...] = lanes_dot(order[...], active[...].reshape(-1, CH)).astype(BF16)

    first = core[0] * (TAPS - 1) + 2 * step

    def window(tap):
        time_tap = lax.div(tap, 9)
        rest = tap - 9 * time_tap
        row_tap = lax.div(rest, 3)
        col_tap = rest - 3 * row_tap
        return windows[time_tap, pl.ds(2 - row_tap, 2), pl.ds(2 - col_tap, COLS)].reshape(-1, CH)

    right = jnp.concatenate([window(first), window(first + 1)], axis=1)
    product = jnp.dot(turned[...], right, preferred_element_type=F32).astype(BF16)
    for part, out in enumerate((out0, out1, out2, out3)):
        for which in range(2):
            out[which] = product[part * 96 : (part + 1) * 96, which * CH : (which + 1) * CH]


def weight_grad(core, own, low, high, feats, own2, low2, high2, feats2, order):
    whole = lambda shape: pl.BlockSpec(shape, lambda i: (0,) * len(shape))
    rows = [whole((2, COLS, SPAN, CH)), whole((COLS, SPAN, CH)), whole((COLS, SPAN, CH)),
            whole((2, COLS, SPAN, CH))]
    return pl.pallas_call(
        weight_kernel,
        grid=(TAPS // 2,),
        in_specs=[pl.BlockSpec(memory_space=pltpu.SMEM), *rows, *rows, whole((CH, CH))],
        out_specs=[pl.BlockSpec((2, 96, CH), lambda i: (i, 0, 0))] * 4,
        out_shape=[jax.ShapeDtypeStruct((TAPS, 96, CH), BF16)] * 4,
        scratch_shapes=[
            pltpu.VMEM((3, 4, COLS + 2, 2 * SPAN, CH), BF16),
            pltpu.VMEM((2, COLS, 2 * SPAN, CH), BF16),
            pltpu.VMEM((CH, 2 * COLS * 2 * SPAN), BF16),
        ],
        compiler_params=pltpu.CompilerParams(vmem_limit_bytes=VMEM),
        cost_estimate=pl.CostEstimate(
            flops=2 * 1536 * TAPS * CH * CH, bytes_accessed=12_000_000, transcendentals=1536 * CH
        ),
        name="weight_grad",
    )(core, own, low, high, feats, own2, low2, high2, feats2, order)


def stats_kernel(states, mods, head_input, mean, inv):
    values = states[...].astype(F32)
    average = jnp.mean(values, axis=-1, keepdims=True)
    centered = values - average
    inv_std = lax.rsqrt(jnp.mean(centered * centered, axis=-1, keepdims=True) + 1e-06)
    head_input[...] = (centered * inv_std * (1.0 + mods[1:2, :]) + mods[0:1, :]).astype(BF16)
    mean[...] = jnp.broadcast_to(average, mean.shape)
    inv[...] = jnp.broadcast_to(inv_std, inv.shape)


def stats(states, mods):
    tokens = states.shape[0]
    return pl.pallas_call(
        stats_kernel,
        grid=(tokens // 32,),
        in_specs=[
            pl.BlockSpec((32, WIDTH), lambda i: (i, 0)),
            pl.BlockSpec((2, WIDTH), lambda i: (0, 0)),
        ],
        out_specs=[
            pl.BlockSpec((32, WIDTH), lambda i: (i, 0)),
            pl.BlockSpec((32, 128), lambda i: (i, 0)),
            pl.BlockSpec((32, 128), lambda i: (i, 0)),
        ],
        out_shape=[
            jax.ShapeDtypeStruct((tokens, WIDTH), BF16),
            jax.ShapeDtypeStruct((tokens, 128), F32),
            jax.ShapeDtypeStruct((tokens, 128), F32),
        ],
        compiler_params=pltpu.CompilerParams(vmem_limit_bytes=VMEM),
        cost_estimate=pl.CostEstimate(
            flops=10_000_000, bytes_accessed=4_000_000, transcendentals=192
        ),
        name="token_stats",
    )(states, mods)


def head_kernel(
    sent, states, head_input, head_weight, mods, mean, inv,
    load, patch_out, sum_out, dot_out, patch, patch_t, gains, piece, sums, dots,
):
    step = pl.program_id(0)
    tokens = patch.shape[0]

    @pl.when(step == 0)
    def _():
        below = lax.broadcasted_iota(jnp.int32, (SPAN, 128), 0)
        lane = lax.broadcasted_iota(jnp.int32, (SPAN, 128), 1)
        parts = []
        for pair in range(6):
            here = sent[:, pair * 128 : (pair + 1) * 128]
            swapped = pltpu.roll(here, 64, 1)
            before = jnp.where(below > 0, pltpu.roll(swapped, 1, 0), 0.0)
            after = jnp.where(below < SPAN - 1, pltpu.roll(swapped, SPAN - 1, 0), 0.0)
            summed = here + jnp.where(lane < 64, before, after)
            inside = (lane >= 32) & (lane < 96)
            parts.append(jnp.where(inside, summed, 0.0).astype(BF16))
        stacked = jnp.concatenate(parts, axis=0)
        token = lax.broadcasted_iota(jnp.int32, (tokens, tokens), 0)
        source = lax.broadcasted_iota(jnp.int32, (tokens, tokens), 1)
        match = (source & (SPAN - 1)) * 6 + lax.shift_right_logical(source, 5) == token
        pick = jnp.where(match, 1.0, 0.0).astype(BF16)
        ordered = jnp.dot(pick, stacked, preferred_element_type=F32)
        patch[...] = ordered.astype(BF16)
        patch_out[...] = ordered.astype(BF16)
        patch_t[...] = ordered.T.astype(BF16)
        sums[...] = jnp.zeros_like(sums)
        dots[...] = jnp.zeros_like(dots)
        piece[...] = jnp.zeros_like(piece)

    grad = lanes_dot(patch[...], head_weight[...])
    normed = (states[...].astype(F32) - mean[:, 0:1]) * inv[:, 0:1]
    weighted = grad * normed
    at = pl.multiple_of(step * STEP, STEP)
    gains[0:1, pl.ds(at, STEP)] = jnp.sum(grad, axis=0, keepdims=True)
    gains[1:2, pl.ds(at, STEP)] = jnp.sum(weighted, axis=0, keepdims=True)
    scale = 1.0 + mods[1:2, :]
    sums[...] += jnp.sum(grad * scale, axis=-1, keepdims=True)
    dots[...] += jnp.sum(weighted * scale, axis=-1, keepdims=True)
    product = jnp.dot(patch_t[...], head_input[...], preferred_element_type=F32)
    half = lax.div(step, 5)
    lanes = pl.multiple_of((step - 5 * half) * STEP, STEP)
    load[pl.ds(pl.multiple_of(half * 64, 64), 64), pl.ds(lanes, STEP)] = product[32:96].astype(BF16)

    @pl.when(step == pl.num_programs(0) - 1)
    def _():
        for block in range(80):
            row, lane = divmod(block, 40)
            piece[block // 3 : block // 3 + 1, pl.ds((block % 3) * 128, 128)] = gains[
                row : row + 1, lane * 128 : (lane + 1) * 128
            ]
        narrow = piece[...].astype(BF16)
        for group in range(4):
            load[group * 32 : (group + 1) * 32, HALF:LOAD] = narrow
        sum_out[...] = sums[...] * (1.0 / WIDTH)
        dot_out[...] = dots[...] * (1.0 / WIDTH)


def head_sums(sent, states, head_input, head_weight, mods, mean, inv):
    tokens = states.shape[0]
    fixed = lambda shape: pl.BlockSpec(shape, lambda i: (0, 0))
    return pl.pallas_call(
        head_kernel,
        grid=(WIDTH // STEP,),
        in_specs=[
            fixed((SPAN, 768)),
            pl.BlockSpec((tokens, STEP), lambda i: (0, i)),
            pl.BlockSpec((tokens, STEP), lambda i: (0, i)),
            pl.BlockSpec((STEP, 128), lambda i: (i, 0)),
            pl.BlockSpec((2, STEP), lambda i: (0, i)),
            fixed((tokens, 128)),
            fixed((tokens, 128)),
        ],
        out_specs=[fixed((128, LOAD)), fixed((tokens, 128)), fixed((tokens, 128)),
                   fixed((tokens, 128))],
        out_shape=[
            jax.ShapeDtypeStruct((128, LOAD), BF16),
            jax.ShapeDtypeStruct((tokens, 128), BF16),
            jax.ShapeDtypeStruct((tokens, 128), F32),
            jax.ShapeDtypeStruct((tokens, 128), F32),
        ],
        scratch_shapes=[
            pltpu.VMEM((tokens, 128), BF16),
            pltpu.VMEM((128, tokens), BF16),
            pltpu.VMEM((2, WIDTH), F32),
            pltpu.VMEM((32, PIECE), F32),
            pltpu.VMEM((tokens, 128), F32),
            pltpu.VMEM((tokens, 128), F32),
        ],
        compiler_params=pltpu.CompilerParams(vmem_limit_bytes=VMEM),
        cost_estimate=pl.CostEstimate(
            flops=2 * 2 * 192 * 128 * WIDTH, bytes_accessed=7_000_000, transcendentals=0
        ),
        name="head_sums",
    )(sent, states, head_input, head_weight, mods, mean, inv)


def hidden_kernel(patch, states, head_weight, mods, mean, inv, sums, dots, out):
    grad = lanes_dot(patch[...], head_weight[...])
    inv_std = inv[:, 0:1]
    normed = (states[...].astype(F32) - mean[:, 0:1]) * inv_std
    scaled = grad * (1.0 + mods[1:2, :])
    out[...] = ((scaled - sums[:, 0:1] - normed * dots[:, 0:1]) * inv_std).astype(BF16)


def hidden_grads(patch, states, head_weight, mods, mean, inv, sums, dots):
    tokens = states.shape[0]
    fixed = lambda shape: pl.BlockSpec(shape, lambda i: (0, 0))
    return pl.pallas_call(
        hidden_kernel,
        grid=(WIDTH // STEP,),
        in_specs=[
            fixed((tokens, 128)),
            pl.BlockSpec((tokens, STEP), lambda i: (0, i)),
            pl.BlockSpec((STEP, 128), lambda i: (i, 0)),
            pl.BlockSpec((2, STEP), lambda i: (0, i)),
            *[fixed((tokens, 128))] * 4,
        ],
        out_specs=pl.BlockSpec((tokens, STEP), lambda i: (0, i)),
        out_shape=jax.ShapeDtypeStruct((tokens, WIDTH), BF16),
        compiler_params=pltpu.CompilerParams(vmem_limit_bytes=VMEM),
        cost_estimate=pl.CostEstimate(
            flops=2 * 192 * 128 * WIDTH, bytes_accessed=6_000_000, transcendentals=0
        ),
        name="hidden_grads",
    )(patch, states, head_weight, mods, mean, inv, sums, dots)


def channel_order(core, x, z, y_low):
    at = jnp.arange(CH, dtype=jnp.int32)
    first, second, rel, inner = at // 96, (at // 24) % 4, (at // 12) % 2, at % 12
    x_at = (x + jnp.where(core == 0, second, first)) % 4
    z_at = (z + jnp.where(core == 0, first, second)) % 4
    channel = 12 * ((y_low ^ rel) * 16 + x_at * 4 + z_at) + inner
    return (channel[:, None] == jnp.arange(CH, dtype=jnp.int32)[None, :]).astype(BF16)


def added(*terms):
    return functools.reduce(lambda a, b: a + b, [term.astype(F32) for term in terms])


def reduce_weights(parts):
    got = [lax.ppermute(parts[k], BOTH, along(0, k)) for k in (1, 2, 3)]
    summed = added(parts[0], *got).astype(BF16)
    rows = [summed[:, 24 * k : 24 * (k + 1)] for k in range(4)]
    got = [lax.ppermute(rows[k], BOTH, along(1, k)) for k in (1, 2, 3)]
    summed = added(rows[0], *got).astype(BF16)
    same, flipped = summed[:, :12], summed[:, 12:]
    far = lax.ppermute(same, BOTH, along_y(2))
    up = lax.ppermute(flipped, BOTH, along_y(1))
    down = lax.ppermute(flipped, BOTH, along_y(3))
    return added(same, far) + added(up, down)


def local(
    features, pixel_grad, frame_list, conv_weight, in_weight, last_hidden, modulation, head_weight
):
    clips, frames, rows_here, columns, _ = features.shape
    clip = lax.axis_index("clip")
    tile = lax.axis_index("tile")
    _, x, z, core = place(clip, tile)
    y_low = tile // 16

    scored = jnp.any(
        frame_list[:, None, :] == jnp.arange(frames, dtype=jnp.int32)[None, :, None], axis=-1
    )
    masked = pixel_grad * scored.astype(BF16)[:, :, None, None, None]
    own = jnp.transpose(masked, (2, 3, 0, 1, 4)).reshape(rows_here, columns, SPAN, CH)
    feats = jnp.transpose(features, (2, 3, 0, 1, 4)).reshape(rows_here, columns, SPAN, CH)

    up = [(i, i + 1) for i in range(31)]
    down = [(i + 1, i) for i in range(31)]
    low = lax.ppermute(own[1], "tile", up)
    high = lax.ppermute(own[0], "tile", down)
    own2 = lax.ppermute(own, BOTH, OTHER_CORE)
    feats2 = lax.ppermute(feats, BOTH, OTHER_CORE)
    low2 = lax.ppermute(low, BOTH, OTHER_CORE)
    high2 = lax.ppermute(high, BOTH, OTHER_CORE)

    mods = lax.dynamic_index_in_dim(modulation, y_low, 0, keepdims=False)
    head_wide = jnp.pad(head_weight, ((0, 0), (32, 32)))
    head_input, mean, inv = stats(last_hidden, mods)

    sent = input_grad(own, low, high, feats, conv_weight, in_weight)
    parts = weight_grad(
        core.astype(jnp.int32).reshape(1), own, low, high, feats, own2, low2, high2, feats2,
        channel_order(core, x, z, y_low),
    )
    sent = lax.all_to_all(sent, "tile", 0, 0, tiled=True)
    load, patch, sums, dots = head_sums(
        sent, last_hidden, head_input, head_wide, mods, mean, inv
    )
    got = lax.all_to_all(load, BOTH, 0, 0, tiled=True)
    hidden_grad = hidden_grads(patch, last_hidden, head_wide, mods, mean, inv, sums, dots)

    line = jnp.sum(got[:, :HALF].astype(F32), axis=0)
    mine = lax.dynamic_slice_in_dim(got[:, HALF:], clip * 32, 32, 0).astype(F32)
    gains = jnp.sum(mine.reshape(2, 16, PIECE), axis=1).reshape(-1)
    line = jnp.concatenate([line, gains]).astype(BF16)
    back = lax.all_to_all(
        jnp.broadcast_to(line[None], (128, BACK)), BOTH, 0, 0, tiled=True
    )
    head_weight_grad = (
        jnp.transpose(back[:, :HALF].reshape(2, 64, HALF), (0, 2, 1))
        .reshape(WIDTH, 64)
        .astype(F32)
    )
    gains = lax.dynamic_slice_in_dim(back[:, HALF:], clip * 32, 32, 0).astype(F32)
    modulation_grad = (
        jnp.transpose(gains.reshape(32, 2, PIECE), (1, 0, 2))
        .reshape(2, 32 * PIECE)[:, : 2 * WIDTH]
        .reshape(2, 2, WIDTH)
    )

    share = reduce_weights(parts)
    theirs = lax.ppermute(share, BOTH, OTHER_CORE)
    conv_weight_grad = jnp.where(
        core == 0,
        jnp.concatenate([share, theirs[1:]], axis=0),
        jnp.concatenate([theirs, share[1:]], axis=0),
    ).reshape(3, 3, 3, 12, CH)
    return (hidden_grad, head_weight_grad, modulation_grad, conv_weight_grad)


def solution(mesh):
    return jax.shard_map(
        local,
        mesh=mesh,
        in_specs=(
            P("clip", None, "tile", None, None),
            P("clip", None, "tile", None, None),
            P("clip", None),
            P(),
            P(),
            P(("clip", "tile"), None),
            P("clip", None, None),
            P(),
        ),
        out_specs=(
            P(("clip", "tile"), None),
            P(),
            P("clip", None, None),
            P(None, None, None, "tile", None),
        ),
        check_vma=False,
    )
```

```python
import functools

import jax
import jax.numpy as jnp
from jax import lax
from jax.experimental import pallas as pl
from jax.experimental.pallas import tpu as pltpu
from jax.sharding import PartitionSpec as P

F32 = jnp.float32
BF16 = jnp.bfloat16
BOTH = ("clip", "tile")
FRAMES = 16
SPAN = 32
COLS = 12
CH = 384
WIDTH = 5120
HALF = 2560
STEP = 1280
TAPS = 14
LARGE = 56 * 1024 * 1024
IN_VMEM = pl.BlockSpec(memory_space=pltpu.VMEM)


def place(clip, tile):
    return (clip // 2) * 2 + tile // 16, (tile // 4) % 4, tile % 4, clip % 2


def number(y, x, z, core):
    return ((y // 2) * 2 + core) * 32 + (y % 2) * 16 + x * 4 + z


def pairs(shift_of):
    out = []
    for source in range(128):
        where = place(source // 32, source % 32)
        out.append((source, number(*shift_of(*where))))
    return out


def along(core_axis, steps):
    def shift(y, x, z, core):
        if core == core_axis:
            return y, x, (z + steps) % 4, core
        return y, (x + steps) % 4, z, core

    return pairs(shift)


def along_y(steps):
    return pairs(lambda y, x, z, core: ((y + steps) % 4, x, z, core))


SAME_CORE = [[c * 32 + t for c in (core, core + 2) for t in range(32)] for core in (0, 1)]
OTHER_CORE = pairs(lambda y, x, z, core: (y, x, z, 1 - core))


def shift_frames(tile, steps):
    if steps == 0:
        return tile
    count = tile.shape[0]
    moved = pltpu.roll(tile, count - steps, 0)
    frame = lax.broadcasted_iota(jnp.int32, tile.shape, 0) & (FRAMES - 1)
    return jnp.where(frame < FRAMES - steps, moved, 0.0)


def fill_row(padded, source, base, keep=None):
    blank = jnp.zeros((SPAN, CH), BF16)
    padded[0, pl.ds(base, SPAN)] = blank
    padded[COLS + 1, pl.ds(base, SPAN)] = blank
    rows = source[...]
    padded[pl.ds(1, COLS), pl.ds(base, SPAN)] = rows if keep is None else rows * keep[...]


def lanes_dot(left, right):
    return lax.dot_general(left, right, (((1,), (1,)), ((), ())), preferred_element_type=F32)


def column_windows(rows):
    return jnp.concatenate(
        [rows[:, 2 - col_tap : 2 - col_tap + COLS].reshape(-1, CH) for col_tap in range(3)], axis=1
    )


def tap_weights(weight):
    return jnp.concatenate(
        [
            jnp.concatenate([weight[time_tap, 0, col_tap] for col_tap in range(3)], axis=1)
            for time_tap in range(3)
        ],
        axis=0,
    )


def grad_kernel(
    own, low, high, keep, feats, weight, in_weight, out, padded, total, grads, spread
):
    step = pl.program_id(0)

    @pl.when(step == 0)
    def _():
        for row, source in enumerate((low, own.at[0], own.at[1], high)):
            fill_row(padded.at[row], source, 0, None if row in (1, 2) else keep)
        total[...] = lanes_dot(column_windows(padded.at[1:3]), tap_weights(weight))
        blank = jnp.zeros((16, CH), BF16)
        for time_tap in range(3):
            for rowout in range(4):
                for parity in range(2):
                    at = ((time_tap * 4 + rowout) * 2 + parity) * 16
                    for near in range(4):
                        for side in range(2):
                            row_tap = rowout - side
                            col_tap = parity + 2 - near
                            inside = 0 <= row_tap <= 2 and 0 <= col_tap <= 2
                            value = in_weight[time_tap, row_tap, col_tap] if inside else blank
                            spread[at : at + 16, pl.ds((near * 2 + side) * CH, CH)] = value

    @pl.when(step == 1)
    def _():
        total[...] += lanes_dot(column_windows(padded.at[2:4]), tap_weights(weight))

    def finish(side, source):
        blank = jnp.zeros((SPAN, CH), BF16)
        grads[side, 0, 0] = blank
        grads[side, 6, 1] = blank
        for col in range(COLS):
            values = feats[side, col].astype(F32)
            sig = jax.nn.sigmoid(values)
            slope = sig * (1.0 + values * (1.0 - sig))
            tile = source[col * SPAN : (col + 1) * SPAN]
            summed = (
                tile[:, 0:CH]
                + shift_frames(tile[:, CH : 2 * CH], 1)
                + shift_frames(tile[:, 2 * CH : 3 * CH], 2)
            )
            grads[side, (col + 1) // 2, (col + 1) % 2] = (summed * slope).astype(BF16)

    @pl.when(step == 2)
    def _():
        total[...] += lanes_dot(column_windows(padded.at[0:2]), tap_weights(weight))
        for side in range(2):
            finish(side, total.at[side * 384 : (side + 1) * 384])
        left = jnp.concatenate(
            [
                grads[side, pl.ds(near // 2, 6), near % 2].reshape(-1, CH)
                for near in range(4)
                for side in range(2)
            ],
            axis=1,
        )
        latent = lanes_dot(left, spread[...])
        for pair in range(6):
            block = latent[pair * SPAN : (pair + 1) * SPAN]
            out[:, pair, :] = (
                block[:, 0:128]
                + shift_frames(block[:, 128:256], 1)
                + shift_frames(block[:, 256:384], 2)
            )
        out[:, 6:8, :] = jnp.zeros((SPAN, 2, 128), F32)


def whole(*shape):
    return pl.BlockSpec(shape, lambda i: (0,) * len(shape))


def input_grad(own, low, high, keep, feats, conv_weight, in_weight):
    return pl.pallas_call(
        grad_kernel,
        grid=(3,),
        in_specs=[
            whole(2, COLS, SPAN, CH),
            whole(COLS, SPAN, CH),
            whole(COLS, SPAN, CH),
            whole(SPAN, CH),
            whole(2, COLS, SPAN, CH),
            pl.BlockSpec((3, 1, 3, CH, CH), lambda i: (0, jnp.where(i == 2, 2, 1 - i), 0, 0, 0)),
            whole(3, 3, 3, 16, CH),
        ],
        out_specs=whole(SPAN, 8, 128),
        out_shape=jax.ShapeDtypeStruct((SPAN, 8, 128), F32),
        scratch_shapes=[
            pltpu.VMEM((4, COLS + 2, SPAN, CH), BF16),
            pltpu.VMEM((2 * COLS * SPAN, 3 * CH), F32),
            pltpu.VMEM((2, 7, 2, SPAN, CH), BF16),
            pltpu.VMEM((384, 8 * CH), BF16),
        ],
        compiler_params=pltpu.CompilerParams(vmem_limit_bytes=LARGE),
        cost_estimate=pl.CostEstimate(
            flops=2 * 768 * 27 * CH * CH, bytes_accessed=12_000_000, transcendentals=768 * CH
        ),
        name="input_grad",
    )(own, low, high, keep, feats, conv_weight, in_weight)


def weight_kernel(
    core, own, low, high, keep, feats, own2, low2, high2, keep2, feats2, order,
    out0, out1, out2, out3, padded, active, turned,
):
    step = pl.program_id(0)

    @pl.when(step == 0)
    def _():
        for base, rows, kept in ((0, (low, own.at[0], own.at[1], high), keep),
                                 (SPAN, (low2, own2.at[0], own2.at[1], high2), keep2)):
            for row, source in enumerate(rows):
                fill_row(padded.at[row], source, base, None if row in (1, 2) else kept)
        for base, source in ((0, feats), (SPAN, feats2)):
            for side in range(2):

                def column(col, carry, base=base, source=source, side=side):
                    values = jax.nn.silu(source[side, col].astype(F32))
                    active[side, col, pl.ds(base, SPAN)] = values.astype(BF16)
                    return carry

                lax.fori_loop(0, COLS, column, 0)
        frame = lax.broadcasted_iota(jnp.int32, (CH, 128), 1) & (FRAMES - 1)
        across = lanes_dot(order[...], active[...].reshape(-1, CH))
        for at in range(0, 2 * COLS * 2 * SPAN, 128):
            values = across[:, at : at + 128]
            one = jnp.where(frame >= 1, pltpu.roll(values, 1, 1), 0.0)
            two = jnp.where(frame >= 2, pltpu.roll(values, 2, 1), 0.0)
            turned[0, :, at : at + 128] = jnp.where(core[0] == 0, values, two).astype(BF16)
            turned[1, :, at : at + 128] = one.astype(BF16)

    def window(place_at):
        tap = jnp.where(place_at < 9, place_at, place_at - 9 + 4 * core[0])
        row_tap = lax.div(tap, 3)
        col_tap = tap - 3 * row_tap
        return padded[pl.ds(2 - row_tap, 2), pl.ds(2 - col_tap, COLS)].reshape(-1, CH)

    def write(which, product):
        for part, out in enumerate((out0, out1, out2, out3)):
            out[which] = product[part * 96 : (part + 1) * 96].astype(BF16)

    @pl.when(step != 4)
    def _():
        right = jnp.concatenate([window(2 * step), window(2 * step + 1)], axis=1)
        slot = jnp.where(step < 4, 0, 1)
        product = jnp.dot(turned[slot], right, preferred_element_type=F32)
        write(0, product[:, 0:CH])
        write(1, product[:, CH : 2 * CH])

    @pl.when(step == 4)
    def _():
        for slot in range(2):
            write(slot, jnp.dot(turned[slot], window(8 + slot), preferred_element_type=F32))


def weight_grad(core, own, low, high, keep, feats, own2, low2, high2, keep2, feats2, order):
    rows = [whole(2, COLS, SPAN, CH), whole(COLS, SPAN, CH), whole(COLS, SPAN, CH),
            whole(SPAN, CH), whole(2, COLS, SPAN, CH)]
    return pl.pallas_call(
        weight_kernel,
        grid=(TAPS // 2,),
        in_specs=[pl.BlockSpec(memory_space=pltpu.SMEM), *rows, *rows, whole(CH, CH)],
        out_specs=[pl.BlockSpec((2, 96, CH), lambda i: (i, 0, 0))] * 4,
        out_shape=[jax.ShapeDtypeStruct((TAPS, 96, CH), BF16)] * 4,
        scratch_shapes=[
            pltpu.VMEM((4, COLS + 2, 2 * SPAN, CH), BF16),
            pltpu.VMEM((2, COLS, 2 * SPAN, CH), BF16),
            pltpu.VMEM((2, CH, 2 * COLS * 2 * SPAN), BF16),
        ],
        compiler_params=pltpu.CompilerParams(vmem_limit_bytes=LARGE),
        cost_estimate=pl.CostEstimate(
            flops=2 * 1536 * TAPS * CH * CH, bytes_accessed=12_000_000, transcendentals=1536 * CH
        ),
        name="weight_grad",
    )(core, own, low, high, keep, feats, own2, low2, high2, keep2, feats2, order)


def stats_kernel(states, stat):
    blocks = [slice(at, at + 128) for at in range(0, WIDTH, 128)]
    summed = jnp.zeros((32, 128), F32)
    for block in blocks:
        summed = summed + states[:, block].astype(F32)
    average = jnp.sum(summed, axis=-1, keepdims=True) * (1.0 / WIDTH)
    spread = jnp.broadcast_to(average, (32, 128))
    summed = jnp.zeros((32, 128), F32)
    for block in blocks:
        centered = states[:, block].astype(F32) - spread
        summed = summed + centered * centered
    variance = jnp.sum(summed, axis=-1, keepdims=True) * (1.0 / WIDTH)
    inv_std = jnp.broadcast_to(lax.rsqrt(variance + 1e-06), (32, 128))
    stat[:, 0:128] = spread
    stat[:, 128:256] = inv_std


def stats(states):
    tokens = states.shape[0]
    return pl.pallas_call(
        stats_kernel,
        grid=(tokens // 32,),
        in_specs=[pl.BlockSpec((32, WIDTH), lambda i: (i, 0))],
        out_specs=pl.BlockSpec((32, 256), lambda i: (i, 0)),
        out_shape=jax.ShapeDtypeStruct((tokens, 256), F32),
        compiler_params=pltpu.CompilerParams(vmem_limit_bytes=8 * 1024 * 1024),
        cost_estimate=pl.CostEstimate(flops=1, bytes_accessed=1, transcendentals=0),
        name="token_stats",
    )(states)


def head_kernel(
    core, sent, states, head_weight, mods, stat,
    load, give, terms, patch, patch_t, total, gains, whole, piece, sums, dots,
):
    step = pl.program_id(0)
    tokens = patch.shape[0]

    @pl.when(step == 0)
    def _():
        below = lax.broadcasted_iota(jnp.int32, (SPAN, 128), 0)
        lane = lax.broadcasted_iota(jnp.int32, (SPAN, 128), 1)
        parts = []
        for pair in range(6):
            here = sent[:, pair, :]
            swapped = pltpu.roll(here, 64, 1)
            before = jnp.where(below > 0, pltpu.roll(swapped, 1, 0), 0.0)
            after = jnp.where(below < SPAN - 1, pltpu.roll(swapped, SPAN - 1, 0), 0.0)
            summed = here + jnp.where(lane < 64, before, after)
            inside = (lane >= 32) & (lane < 96)
            parts.append(jnp.where(inside, summed, 0.0).astype(BF16))
        stacked = jnp.concatenate(parts, axis=0)
        token = lax.broadcasted_iota(jnp.int32, (tokens, tokens), 0)
        source = lax.broadcasted_iota(jnp.int32, (tokens, tokens), 1)
        match = (source & (SPAN - 1)) * 6 + lax.shift_right_logical(source, 5) == token
        pick = jnp.where(match, 1.0, 0.0).astype(BF16)
        ordered = jnp.dot(pick, stacked, preferred_element_type=F32)
        patch[...] = ordered[:, 32:96].astype(BF16)
        terms[:, 256:384] = jnp.concatenate([ordered[:, 32:96], ordered[:, 32:96]], axis=1)
        patch_t[...] = ordered.T[32:96].astype(BF16)
        whole[...] = jnp.broadcast_to(jnp.sum(ordered, axis=0, keepdims=True), whole.shape)
        sums[...] = jnp.zeros_like(sums)
        dots[...] = jnp.zeros_like(dots)
        piece[...] = jnp.zeros_like(piece)

    grad = jnp.dot(patch[...], head_weight[...], preferred_element_type=F32)
    normed = (states[...].astype(F32) - stat[:, 0:1]) * stat[:, 128:129]
    weighted = grad * normed
    at = pl.multiple_of(step * STEP, STEP)
    gains[0:1, pl.ds(at, STEP)] = jnp.sum(weighted, axis=0, keepdims=True)
    scale = 1.0 + mods[1:2, :]
    sums[...] += jnp.sum(grad * scale, axis=-1, keepdims=True)
    dots[...] += jnp.sum(weighted * scale, axis=-1, keepdims=True)
    head_input = (normed * scale + mods[0:1, :]).astype(BF16)
    total[:, pl.ds(at, STEP)] = jnp.dot(patch_t[...], head_input, preferred_element_type=F32)

    @pl.when(step == pl.num_programs(0) - 1)
    def _():
        for block in range(40):
            piece[block // 2 : block // 2 + 1, pl.ds((block % 2) * 128, 128)] = gains[
                0:1, block * 128 : (block + 1) * 128
            ]
        extra = jnp.concatenate([piece[...], whole[...], jnp.zeros((32, 128), F32)], axis=1)
        extra = jnp.concatenate([extra, extra], axis=0)
        for out, half in ((load, core[0]), (give, 1 - core[0])):
            rows = total[:, pl.ds(pl.multiple_of(half * HALF, 128), HALF)]
            rows = jnp.concatenate([rows, extra if out is load else extra * 0.0], axis=1)
            out[...] = rows.reshape(64, 24, 128).astype(BF16)
        terms[:, 0:128] = sums[...] * (1.0 / WIDTH)
        terms[:, 128:256] = dots[...] * (1.0 / WIDTH)


def head_sums(core, sent, states, head_weight, mods, stat):
    tokens = states.shape[0]
    fixed = lambda *shape: pl.BlockSpec(shape, lambda i: (0,) * len(shape))
    return pl.pallas_call(
        head_kernel,
        grid=(WIDTH // STEP,),
        in_specs=[
            pl.BlockSpec(memory_space=pltpu.SMEM),
            fixed(SPAN, 8, 128),
            pl.BlockSpec((tokens, STEP), lambda i: (0, i)),
            pl.BlockSpec((64, STEP), lambda i: (0, i)),
            pl.BlockSpec((2, STEP), lambda i: (0, i)),
            fixed(tokens, 256),
        ],
        out_specs=[fixed(64, 24, 128), fixed(64, 24, 128), fixed(tokens, 384)],
        out_shape=[
            jax.ShapeDtypeStruct((64, 24, 128), BF16),
            jax.ShapeDtypeStruct((64, 24, 128), BF16),
            jax.ShapeDtypeStruct((tokens, 384), F32),
        ],
        scratch_shapes=[
            pltpu.VMEM((tokens, 64), BF16),
            pltpu.VMEM((64, tokens), BF16),
            pltpu.VMEM((64, WIDTH), F32),
            pltpu.VMEM((1, WIDTH), F32),
            pltpu.VMEM((32, 128), F32),
            pltpu.VMEM((32, 256), F32),
            pltpu.VMEM((tokens, 128), F32),
            pltpu.VMEM((tokens, 128), F32),
        ],
        compiler_params=pltpu.CompilerParams(vmem_limit_bytes=32 * 1024 * 1024),
        cost_estimate=pl.CostEstimate(
            flops=2 * 2 * 192 * 128 * WIDTH, bytes_accessed=7_000_000, transcendentals=0
        ),
        name="head_sums",
    )(core, sent, states, head_weight, mods, stat)


def combine_kernel(y_high, got, back, whole):
    def add(at, carry):
        for near in range(8):
            carry = carry + got[at * 8 + near].astype(F32)
        return carry

    total = lax.fori_loop(0, 8, add, jnp.zeros((24, 128), F32))
    mine = []
    for y_low in range(2):
        summed = jnp.zeros((24, 128), F32)
        for near in range(16):
            summed = summed + got[y_high[0] * 32 + y_low * 16 + near].astype(F32)
        mine.append(summed)
    row = lax.broadcasted_iota(jnp.int32, (24, 128), 0)
    line = jnp.where(row < 20, total, jnp.where(row < 22, mine[0], pltpu.roll(mine[1], 2, 0)))
    back[...] = jnp.broadcast_to(line.astype(BF16)[None], back.shape)
    whole[...] = jnp.zeros_like(whole)
    whole[0:1] = mine[0][22:23]
    whole[1:2] = mine[1][22:23]


def combine(y_high, got):
    return pl.pallas_call(
        combine_kernel,
        in_specs=[
            pl.BlockSpec(memory_space=pltpu.SMEM),
            pl.BlockSpec(memory_space=pltpu.VMEM),
        ],
        out_specs=[pl.BlockSpec(memory_space=pltpu.VMEM)] * 2,
        out_shape=[
            jax.ShapeDtypeStruct((64, 24, 128), BF16),
            jax.ShapeDtypeStruct((8, 128), F32),
        ],
        compiler_params=pltpu.CompilerParams(vmem_limit_bytes=16 * 1024 * 1024),
        cost_estimate=pl.CostEstimate(
            flops=1_000_000, bytes_accessed=1_600_000, transcendentals=0
        ),
        name="combine",
    )(y_high, got)


def unpack_kernel(place_at, back, theirs, whole, head_weight, weights, mods):
    for source, half in ((back, place_at[0]), (theirs, 1 - place_at[0])):
        rows = source[...].astype(F32).reshape(64, 24 * 128)
        weights[:, pl.ds(pl.multiple_of(half * HALF, 128), HALF)] = rows[:, 0:HALF]
    summed = whole[:, 32:96]
    high = summed.astype(BF16)
    low = (summed - high.astype(F32)).astype(BF16)
    shifts = jnp.dot(high, head_weight[...], preferred_element_type=F32) + jnp.dot(
        low, head_weight[...], preferred_element_type=F32
    )
    for y_low in range(2):
        mods[y_low, 0:1, :] = shifts[y_low : y_low + 1]
    for part in range(20):
        rows = back[place_at[1] * 32 + part].astype(F32)
        for y_low in range(2):
            for near in range(2):
                at = (2 * part + near) * 128
                row = 20 + 2 * y_low + near
                mods[y_low, 1:2, at : at + 128] = rows[row : row + 1]


def unpack(place_at, back, theirs, whole, head_weight):
    return pl.pallas_call(
        unpack_kernel,
        in_specs=[pl.BlockSpec(memory_space=pltpu.SMEM)]
        + [pl.BlockSpec(memory_space=pltpu.VMEM)] * 4,
        out_specs=[pl.BlockSpec(memory_space=pltpu.VMEM)] * 2,
        out_shape=[
            jax.ShapeDtypeStruct((64, WIDTH), F32),
            jax.ShapeDtypeStruct((2, 2, WIDTH), F32),
        ],
        compiler_params=pltpu.CompilerParams(vmem_limit_bytes=24 * 1024 * 1024),
        cost_estimate=pl.CostEstimate(
            flops=10_000_000, bytes_accessed=3_000_000, transcendentals=0
        ),
        name="unpack",
    )(place_at, back, theirs, whole, head_weight)


def hidden_kernel(terms, states, head_weight, mods, stat, out):
    patch = terms[:, 256:320].astype(BF16)
    grad = jnp.dot(patch, head_weight[...], preferred_element_type=F32)
    inv_std = stat[:, 128:129]
    normed = (states[...].astype(F32) - stat[:, 0:1]) * inv_std
    scaled = grad * (1.0 + mods[1:2, :])
    out[...] = ((scaled - terms[:, 0:1] - normed * terms[:, 128:129]) * inv_std).astype(BF16)


def hidden_grads(terms, states, head_weight, mods, stat):
    tokens = states.shape[0]
    fixed = lambda *shape: pl.BlockSpec(shape, lambda i: (0, 0))
    return pl.pallas_call(
        hidden_kernel,
        grid=(WIDTH // STEP,),
        in_specs=[
            fixed(tokens, 384),
            pl.BlockSpec((tokens, STEP), lambda i: (0, i)),
            pl.BlockSpec((64, STEP), lambda i: (0, i)),
            pl.BlockSpec((2, STEP), lambda i: (0, i)),
            fixed(tokens, 256),
        ],
        out_specs=pl.BlockSpec((tokens, STEP), lambda i: (0, i)),
        out_shape=jax.ShapeDtypeStruct((tokens, WIDTH), BF16),
        compiler_params=pltpu.CompilerParams(vmem_limit_bytes=LARGE),
        cost_estimate=pl.CostEstimate(flops=1, bytes_accessed=1, transcendentals=0),
        name="hidden_grads",
    )(terms, states, head_weight, mods, stat)


def channel_order(core, x, z, y_low):
    at = jnp.arange(CH, dtype=jnp.int32)
    first, second, rel, inner = at // 96, (at // 24) % 4, (at // 12) % 2, at % 12
    x_at = (x + jnp.where(core == 0, second, first)) % 4
    z_at = (z + jnp.where(core == 0, first, second)) % 4
    channel = 12 * ((y_low ^ rel) * 16 + x_at * 4 + z_at) + inner
    return (channel[:, None] == jnp.arange(CH, dtype=jnp.int32)[None, :]).astype(BF16)


def sum_kernel(first, second, third, fourth, *outs):
    rows = outs[0].shape[1]
    for tap in range(first.shape[0]):
        total = (first[tap].astype(F32) + second[tap].astype(F32)) + (
            third[tap].astype(F32) + fourth[tap].astype(F32)
        )
        for part, out in enumerate(outs):
            out[tap] = total[part * rows : (part + 1) * rows].astype(BF16)


def sum_parts(terms, count):
    taps, rows, _ = terms[0].shape
    block = lambda height: pl.BlockSpec((taps // 2, height, CH), lambda i: (i, 0, 0))
    return pl.pallas_call(
        sum_kernel,
        grid=(2,),
        in_specs=[block(rows)] * 4,
        out_specs=[block(rows // count)] * count,
        out_shape=[jax.ShapeDtypeStruct((taps, rows // count, CH), BF16)] * count,
        compiler_params=pltpu.CompilerParams(vmem_limit_bytes=LARGE),
        cost_estimate=pl.CostEstimate(flops=1, bytes_accessed=1, transcendentals=0),
        name="sum_parts",
    )(*terms)


def added(*terms):
    return functools.reduce(lambda a, b: a + b, [term.astype(F32) for term in terms])


def local(
    features, pixel_grad, frame_list, conv_weight, in_weight, last_hidden, modulation, head_weight
):
    clips, frames, rows_here, columns, _ = features.shape
    clip = lax.axis_index("clip")
    tile = lax.axis_index("tile")
    _, x, z, core = place(clip, tile)
    y_low = tile // 16

    up = [(i, i + 1) for i in range(31)]
    down = [(i + 1, i) for i in range(31)]
    border = [
        jnp.transpose(pixel_grad[:, :, row], (2, 0, 1, 3)).reshape(columns, SPAN, CH)
        for row in (0, 1)
    ]
    low = lax.ppermute(border[1], "tile", up)
    high = lax.ppermute(border[0], "tile", down)

    scored = jnp.any(
        frame_list[:, None, :] == jnp.arange(frames, dtype=jnp.int32)[None, :, None], axis=-1
    ).astype(BF16)
    keep = jnp.broadcast_to(scored.reshape(SPAN, 1), (SPAN, CH))
    masked = pixel_grad * scored[:, :, None, None, None]
    own = jnp.transpose(masked, (2, 3, 0, 1, 4)).reshape(rows_here, columns, SPAN, CH)
    feats = jnp.transpose(features, (2, 3, 0, 1, 4)).reshape(rows_here, columns, SPAN, CH)
    own2 = lax.ppermute(own, BOTH, OTHER_CORE)
    feats2 = lax.ppermute(feats, BOTH, OTHER_CORE)
    keep2 = lax.ppermute(keep, BOTH, OTHER_CORE)
    low2 = lax.ppermute(low, BOTH, OTHER_CORE)
    high2 = lax.ppermute(high, BOTH, OTHER_CORE)

    mods = lax.dynamic_index_in_dim(modulation, y_low, 0, keepdims=False)
    head_t = head_weight.T
    core_at = core.astype(jnp.int32).reshape(1)
    y_high = (clip // 2).astype(jnp.int32).reshape(1)
    order = channel_order(core, x, z, y_low)
    parts = weight_grad(
        core_at, own, low, high, keep, feats, own2, low2, high2, keep2, feats2, order
    )
    moved = [lax.ppermute(parts[k], BOTH, along(0, k)) for k in (1, 2, 3)]

    low, high, _ = lax.optimization_barrier((low, high, parts))
    sent = input_grad(own, low, high, keep, feats, conv_weight, in_weight)
    states, _ = lax.optimization_barrier((last_hidden, sent))
    stat = stats(states)
    sent = lax.all_to_all(sent, "tile", 0, 0, tiled=True)
    moved, _ = lax.optimization_barrier((moved, stat))
    rows = sum_parts([parts[0], *moved], 4)
    sent, rows = lax.optimization_barrier((sent, rows))
    moved = [lax.ppermute(rows[k], BOTH, along(1, k)) for k in (1, 2, 3)]

    load, give, terms = head_sums(core_at, sent, last_hidden, head_t, mods, stat)
    give, moved = lax.optimization_barrier((give, moved))
    taken = lax.ppermute(give, BOTH, OTHER_CORE)
    load = added(load, taken).astype(BF16)
    got = lax.all_to_all(load, BOTH, 0, 0, tiled=True, axis_index_groups=SAME_CORE)
    hidden_grad = hidden_grads(terms, last_hidden, head_t, mods, stat)
    same, flipped = sum_parts([rows[0], *moved], 2)
    got, hidden_grad, same, flipped = lax.optimization_barrier((got, hidden_grad, same, flipped))
    far = lax.ppermute(same, BOTH, along_y(2))
    upper = lax.ppermute(flipped, BOTH, along_y(1))
    lower = lax.ppermute(flipped, BOTH, along_y(3))

    back, whole_patch = combine(y_high, got)
    back = lax.all_to_all(back, BOTH, 0, 0, tiled=True, axis_index_groups=SAME_CORE)
    other = lax.ppermute(back, BOTH, OTHER_CORE)
    share = added(same, far) + added(upper, lower)
    weights, modulation_grad = unpack(
        jnp.concatenate([core_at, y_high]), back, other, whole_patch, head_t
    )

    theirs = lax.ppermute(share, BOTH, OTHER_CORE)
    first = jnp.where(core == 0, share, theirs)
    second = jnp.where(core == 0, theirs, share)
    conv_weight_grad = jnp.concatenate([first, second[10:], second[:9]], axis=0)
    return (
        hidden_grad, weights.T, modulation_grad, conv_weight_grad.reshape(3, 3, 3, 12, CH)
    )


def solution(mesh):
    return jax.shard_map(
        local,
        mesh=mesh,
        in_specs=(
            P("clip", None, "tile", None, None),
            P("clip", None, "tile", None, None),
            P("clip", None),
            P(),
            P(),
            P(("clip", "tile"), None),
            P("clip", None, None),
            P(),
        ),
        out_specs=(
            P(("clip", "tile"), None),
            P(),
            P("clip", None, None),
            P(None, None, None, "tile", None),
        ),
        check_vma=False,
    )
```

```python
import functools

import jax
import jax.numpy as jnp
from jax import lax
from jax.experimental import pallas as pl
from jax.experimental.pallas import tpu as pltpu
from jax.sharding import PartitionSpec as P

F32 = jnp.float32
BF16 = jnp.bfloat16
BOTH = ("clip", "tile")
FRAMES = 16
SPAN = 32
COLS = 12
CH = 384
WIDTH = 5120
HALF = 2560
STEP = 1280
TAPS = 14
LARGE = 56 * 1024 * 1024
IN_VMEM = pl.BlockSpec(memory_space=pltpu.VMEM)


def place(clip, tile):
    return (clip // 2) * 2 + tile // 16, (tile // 4) % 4, tile % 4, clip % 2


def number(y, x, z, core):
    return ((y // 2) * 2 + core) * 32 + (y % 2) * 16 + x * 4 + z


def pairs(shift_of):
    out = []
    for source in range(128):
        where = place(source // 32, source % 32)
        out.append((source, number(*shift_of(*where))))
    return out


def along(core_axis, steps):
    def shift(y, x, z, core):
        if core == core_axis:
            return y, x, (z + steps) % 4, core
        return y, (x + steps) % 4, z, core

    return pairs(shift)


def along_y(steps):
    return pairs(lambda y, x, z, core: ((y + steps) % 4, x, z, core))


SAME_CORE = [[c * 32 + t for c in (core, core + 2) for t in range(32)] for core in (0, 1)]
OTHER_CORE = pairs(lambda y, x, z, core: (y, x, z, 1 - core))


def shift_frames(tile, steps):
    if steps == 0:
        return tile
    count = tile.shape[0]
    moved = pltpu.roll(tile, count - steps, 0)
    frame = lax.broadcasted_iota(jnp.int32, tile.shape, 0) & (FRAMES - 1)
    return jnp.where(frame < FRAMES - steps, moved, 0.0)


def fill_row(padded, source, base, keep=None):
    blank = jnp.zeros((SPAN, CH), BF16)
    padded[0, pl.ds(base, SPAN)] = blank
    padded[COLS + 1, pl.ds(base, SPAN)] = blank
    rows = source[...]
    padded[pl.ds(1, COLS), pl.ds(base, SPAN)] = rows if keep is None else rows * keep[...]


def lanes_dot(left, right):
    return lax.dot_general(left, right, (((1,), (1,)), ((), ())), preferred_element_type=F32)


def column_windows(rows):
    return jnp.concatenate(
        [rows[:, 2 - col_tap : 2 - col_tap + COLS].reshape(-1, CH) for col_tap in range(3)], axis=1
    )


def tap_weights(weight):
    return jnp.concatenate(
        [
            jnp.concatenate([weight[time_tap, 0, col_tap] for col_tap in range(3)], axis=1)
            for time_tap in range(3)
        ],
        axis=0,
    )


def grad_kernel(
    own, low, high, keep, feats, weight, in_weight, out, padded, total, grads, spread
):
    step = pl.program_id(0)

    @pl.when(step == 0)
    def _():
        for row, source in enumerate((low, own.at[0], own.at[1], high)):
            fill_row(padded.at[row], source, 0, None if row in (1, 2) else keep)
        total[...] = lanes_dot(column_windows(padded.at[1:3]), tap_weights(weight))
        blank = jnp.zeros((16, CH), BF16)
        for time_tap in range(3):
            for rowout in range(4):
                for parity in range(2):
                    at = ((time_tap * 4 + rowout) * 2 + parity) * 16
                    for near in range(4):
                        for side in range(2):
                            row_tap = rowout - side
                            col_tap = parity + 2 - near
                            inside = 0 <= row_tap <= 2 and 0 <= col_tap <= 2
                            value = in_weight[time_tap, row_tap, col_tap] if inside else blank
                            spread[at : at + 16, pl.ds((near * 2 + side) * CH, CH)] = value

    @pl.when(step == 1)
    def _():
        total[...] += lanes_dot(column_windows(padded.at[2:4]), tap_weights(weight))

    def finish(side, source):
        blank = jnp.zeros((SPAN, CH), BF16)
        grads[side, 0, 0] = blank
        grads[side, 6, 1] = blank
        for col in range(COLS):
            values = feats[side, col].astype(F32)
            sig = jax.nn.sigmoid(values)
            slope = sig * (1.0 + values * (1.0 - sig))
            tile = source[col * SPAN : (col + 1) * SPAN]
            summed = (
                tile[:, 0:CH]
                + shift_frames(tile[:, CH : 2 * CH], 1)
                + shift_frames(tile[:, 2 * CH : 3 * CH], 2)
            )
            grads[side, (col + 1) // 2, (col + 1) % 2] = (summed * slope).astype(BF16)

    @pl.when(step == 2)
    def _():
        total[...] += lanes_dot(column_windows(padded.at[0:2]), tap_weights(weight))
        for side in range(2):
            finish(side, total.at[side * 384 : (side + 1) * 384])
        left = jnp.concatenate(
            [
                grads[side, pl.ds(near // 2, 6), near % 2].reshape(-1, CH)
                for near in range(4)
                for side in range(2)
            ],
            axis=1,
        )
        latent = lanes_dot(left, spread[...])
        for pair in range(6):
            block = latent[pair * SPAN : (pair + 1) * SPAN]
            out[:, pair, :] = (
                block[:, 0:128]
                + shift_frames(block[:, 128:256], 1)
                + shift_frames(block[:, 256:384], 2)
            )
        out[:, 6:8, :] = jnp.zeros((SPAN, 2, 128), F32)


def whole(*shape):
    return pl.BlockSpec(shape, lambda i: (0,) * len(shape))


def input_grad(own, low, high, keep, feats, conv_weight, in_weight):
    return pl.pallas_call(
        grad_kernel,
        grid=(3,),
        in_specs=[
            whole(2, COLS, SPAN, CH),
            whole(COLS, SPAN, CH),
            whole(COLS, SPAN, CH),
            whole(SPAN, CH),
            whole(2, COLS, SPAN, CH),
            pl.BlockSpec((3, 1, 3, CH, CH), lambda i: (0, jnp.where(i == 2, 2, 1 - i), 0, 0, 0)),
            whole(3, 3, 3, 16, CH),
        ],
        out_specs=whole(SPAN, 8, 128),
        out_shape=jax.ShapeDtypeStruct((SPAN, 8, 128), F32),
        scratch_shapes=[
            pltpu.VMEM((4, COLS + 2, SPAN, CH), BF16),
            pltpu.VMEM((2 * COLS * SPAN, 3 * CH), F32),
            pltpu.VMEM((2, 7, 2, SPAN, CH), BF16),
            pltpu.VMEM((384, 8 * CH), BF16),
        ],
        compiler_params=pltpu.CompilerParams(vmem_limit_bytes=LARGE),
        cost_estimate=pl.CostEstimate(
            flops=2 * 768 * 27 * CH * CH, bytes_accessed=12_000_000, transcendentals=768 * CH
        ),
        name="input_grad",
    )(own, low, high, keep, feats, conv_weight, in_weight)


def weight_kernel(
    core, own, low, high, keep, acts, own2, low2, high2, keep2, acts2, order,
    out0, out1, out2, out3, padded, active, turned,
):
    step = pl.program_id(0)

    @pl.when(step == 0)
    def _():
        for base, rows, kept in ((0, (low, own.at[0], own.at[1], high), keep),
                                 (SPAN, (low2, own2.at[0], own2.at[1], high2), keep2)):
            for row, source in enumerate(rows):
                fill_row(padded.at[row], source, base, None if row in (1, 2) else kept)
        for base, source in ((0, acts), (SPAN, acts2)):
            active[:, :, pl.ds(base, SPAN)] = source[...]
        frame = lax.broadcasted_iota(jnp.int32, (CH, 128), 1) & (FRAMES - 1)
        across = lanes_dot(order[...], active[...].reshape(-1, CH))
        for at in range(0, 2 * COLS * 2 * SPAN, 128):
            values = across[:, at : at + 128]
            one = jnp.where(frame >= 1, pltpu.roll(values, 1, 1), 0.0)
            two = jnp.where(frame >= 2, pltpu.roll(values, 2, 1), 0.0)
            turned[0, :, at : at + 128] = jnp.where(core[0] == 0, values, two).astype(BF16)
            turned[1, :, at : at + 128] = one.astype(BF16)

    def window(place_at):
        tap = jnp.where(place_at < 9, place_at, place_at - 9 + 4 * core[0])
        row_tap = lax.div(tap, 3)
        col_tap = tap - 3 * row_tap
        return padded[pl.ds(2 - row_tap, 2), pl.ds(2 - col_tap, COLS)].reshape(-1, CH)

    def write(which, product):
        for part, out in enumerate((out0, out1, out2, out3)):
            out[which] = product[part * 96 : (part + 1) * 96].astype(BF16)

    @pl.when(step != 4)
    def _():
        right = jnp.concatenate([window(2 * step), window(2 * step + 1)], axis=1)
        slot = jnp.where(step < 4, 0, 1)
        product = jnp.dot(turned[slot], right, preferred_element_type=F32)
        write(0, product[:, 0:CH])
        write(1, product[:, CH : 2 * CH])

    @pl.when(step == 4)
    def _():
        for slot in range(2):
            write(slot, jnp.dot(turned[slot], window(8 + slot), preferred_element_type=F32))


def weight_grad(core, own, low, high, keep, acts, own2, low2, high2, keep2, acts2, order):
    rows = [whole(2, COLS, SPAN, CH), whole(COLS, SPAN, CH), whole(COLS, SPAN, CH),
            whole(SPAN, CH), whole(2, COLS, SPAN, CH)]
    return pl.pallas_call(
        weight_kernel,
        grid=(TAPS // 2,),
        in_specs=[pl.BlockSpec(memory_space=pltpu.SMEM), *rows, *rows, whole(CH, CH)],
        out_specs=[pl.BlockSpec((2, 96, CH), lambda i: (i, 0, 0))] * 4,
        out_shape=[jax.ShapeDtypeStruct((TAPS, 96, CH), BF16)] * 4,
        scratch_shapes=[
            pltpu.VMEM((4, COLS + 2, 2 * SPAN, CH), BF16),
            pltpu.VMEM((2, COLS, 2 * SPAN, CH), BF16),
            pltpu.VMEM((2, CH, 2 * COLS * 2 * SPAN), BF16),
        ],
        compiler_params=pltpu.CompilerParams(vmem_limit_bytes=LARGE),
        cost_estimate=pl.CostEstimate(
            flops=2 * 1536 * TAPS * CH * CH, bytes_accessed=12_000_000, transcendentals=1536 * CH
        ),
        name="weight_grad",
    )(core, own, low, high, keep, acts, own2, low2, high2, keep2, acts2, order)


def stats_kernel(states, stat):
    blocks = [slice(at, at + 128) for at in range(0, WIDTH, 128)]
    summed = jnp.zeros((32, 128), F32)
    for block in blocks:
        summed = summed + states[:, block].astype(F32)
    average = jnp.sum(summed, axis=-1, keepdims=True) * (1.0 / WIDTH)
    spread = jnp.broadcast_to(average, (32, 128))
    summed = jnp.zeros((32, 128), F32)
    for block in blocks:
        centered = states[:, block].astype(F32) - spread
        summed = summed + centered * centered
    variance = jnp.sum(summed, axis=-1, keepdims=True) * (1.0 / WIDTH)
    inv_std = jnp.broadcast_to(lax.rsqrt(variance + 1e-06), (32, 128))
    stat[:, 0:128] = spread
    stat[:, 128:256] = inv_std


def stats(states):
    tokens = states.shape[0]
    return pl.pallas_call(
        stats_kernel,
        grid=(tokens // 32,),
        in_specs=[pl.BlockSpec((32, WIDTH), lambda i: (i, 0))],
        out_specs=pl.BlockSpec((32, 256), lambda i: (i, 0)),
        out_shape=jax.ShapeDtypeStruct((tokens, 256), F32),
        compiler_params=pltpu.CompilerParams(vmem_limit_bytes=8 * 1024 * 1024),
        cost_estimate=pl.CostEstimate(flops=1, bytes_accessed=1, transcendentals=0),
        name="token_stats",
    )(states)


def head_kernel(
    core, sent, states, head_weight, mods, stat,
    load, give, terms, patch, patch_t, total, gains, whole, piece, sums, dots,
):
    step = pl.program_id(0)
    tokens = patch.shape[0]

    @pl.when(step == 0)
    def _():
        below = lax.broadcasted_iota(jnp.int32, (SPAN, 128), 0)
        lane = lax.broadcasted_iota(jnp.int32, (SPAN, 128), 1)
        parts = []
        for pair in range(6):
            here = sent[:, pair, :]
            swapped = pltpu.roll(here, 64, 1)
            before = jnp.where(below > 0, pltpu.roll(swapped, 1, 0), 0.0)
            after = jnp.where(below < SPAN - 1, pltpu.roll(swapped, SPAN - 1, 0), 0.0)
            summed = here + jnp.where(lane < 64, before, after)
            inside = (lane >= 32) & (lane < 96)
            parts.append(jnp.where(inside, summed, 0.0).astype(BF16))
        stacked = jnp.concatenate(parts, axis=0)
        token = lax.broadcasted_iota(jnp.int32, (tokens, tokens), 0)
        source = lax.broadcasted_iota(jnp.int32, (tokens, tokens), 1)
        match = (source & (SPAN - 1)) * 6 + lax.shift_right_logical(source, 5) == token
        pick = jnp.where(match, 1.0, 0.0).astype(BF16)
        ordered = jnp.dot(pick, stacked, preferred_element_type=F32)
        patch[...] = ordered[:, 32:96].astype(BF16)
        terms[:, 256:384] = jnp.concatenate([ordered[:, 32:96], ordered[:, 32:96]], axis=1)
        patch_t[...] = ordered.T[32:96].astype(BF16)
        whole[...] = jnp.broadcast_to(jnp.sum(ordered, axis=0, keepdims=True), whole.shape)
        sums[...] = jnp.zeros_like(sums)
        dots[...] = jnp.zeros_like(dots)
        piece[...] = jnp.zeros_like(piece)

    grad = jnp.dot(patch[...], head_weight[...], preferred_element_type=F32)
    normed = (states[...].astype(F32) - stat[:, 0:1]) * stat[:, 128:129]
    weighted = grad * normed
    at = pl.multiple_of(step * STEP, STEP)
    gains[0:1, pl.ds(at, STEP)] = jnp.sum(weighted, axis=0, keepdims=True)
    scale = 1.0 + mods[1:2, :]
    sums[...] += jnp.sum(grad * scale, axis=-1, keepdims=True)
    dots[...] += jnp.sum(weighted * scale, axis=-1, keepdims=True)
    head_input = (normed * scale + mods[0:1, :]).astype(BF16)
    total[:, pl.ds(at, STEP)] = jnp.dot(patch_t[...], head_input, preferred_element_type=F32)

    @pl.when(step == pl.num_programs(0) - 1)
    def _():
        for block in range(40):
            piece[block // 2 : block // 2 + 1, pl.ds((block % 2) * 128, 128)] = gains[
                0:1, block * 128 : (block + 1) * 128
            ]
        extra = jnp.concatenate([piece[...], whole[...], jnp.zeros((32, 128), F32)], axis=1)
        extra = jnp.concatenate([extra, extra], axis=0)
        for out, half in ((load, core[0]), (give, 1 - core[0])):
            rows = total[:, pl.ds(pl.multiple_of(half * HALF, 128), HALF)]
            rows = jnp.concatenate([rows, extra if out is load else extra * 0.0], axis=1)
            out[...] = rows.reshape(64, 24, 128).astype(BF16)
        terms[:, 0:128] = sums[...] * (1.0 / WIDTH)
        terms[:, 128:256] = dots[...] * (1.0 / WIDTH)


def head_sums(core, sent, states, head_weight, mods, stat):
    tokens = states.shape[0]
    fixed = lambda *shape: pl.BlockSpec(shape, lambda i: (0,) * len(shape))
    return pl.pallas_call(
        head_kernel,
        grid=(WIDTH // STEP,),
        in_specs=[
            pl.BlockSpec(memory_space=pltpu.SMEM),
            fixed(SPAN, 8, 128),
            pl.BlockSpec((tokens, STEP), lambda i: (0, i)),
            pl.BlockSpec((64, STEP), lambda i: (0, i)),
            pl.BlockSpec((2, STEP), lambda i: (0, i)),
            fixed(tokens, 256),
        ],
        out_specs=[fixed(64, 24, 128), fixed(64, 24, 128), fixed(tokens, 384)],
        out_shape=[
            jax.ShapeDtypeStruct((64, 24, 128), BF16),
            jax.ShapeDtypeStruct((64, 24, 128), BF16),
            jax.ShapeDtypeStruct((tokens, 384), F32),
        ],
        scratch_shapes=[
            pltpu.VMEM((tokens, 64), BF16),
            pltpu.VMEM((64, tokens), BF16),
            pltpu.VMEM((64, WIDTH), F32),
            pltpu.VMEM((1, WIDTH), F32),
            pltpu.VMEM((32, 128), F32),
            pltpu.VMEM((32, 256), F32),
            pltpu.VMEM((tokens, 128), F32),
            pltpu.VMEM((tokens, 128), F32),
        ],
        compiler_params=pltpu.CompilerParams(vmem_limit_bytes=32 * 1024 * 1024),
        cost_estimate=pl.CostEstimate(
            flops=2 * 2 * 192 * 128 * WIDTH, bytes_accessed=7_000_000, transcendentals=0
        ),
        name="head_sums",
    )(core, sent, states, head_weight, mods, stat)


def combine_kernel(y_high, got, back, whole):
    def add(at, carry):
        for near in range(8):
            carry = carry + got[at * 8 + near].astype(F32)
        return carry

    total = lax.fori_loop(0, 8, add, jnp.zeros((24, 128), F32))
    mine = []
    for y_low in range(2):
        summed = jnp.zeros((24, 128), F32)
        for near in range(16):
            summed = summed + got[y_high[0] * 32 + y_low * 16 + near].astype(F32)
        mine.append(summed)
    row = lax.broadcasted_iota(jnp.int32, (24, 128), 0)
    line = jnp.where(row < 20, total, jnp.where(row < 22, mine[0], pltpu.roll(mine[1], 2, 0)))
    back[...] = jnp.broadcast_to(line.astype(BF16)[None], back.shape)
    whole[...] = jnp.zeros_like(whole)
    whole[0:1] = mine[0][22:23]
    whole[1:2] = mine[1][22:23]


def combine(y_high, got):
    return pl.pallas_call(
        combine_kernel,
        in_specs=[
            pl.BlockSpec(memory_space=pltpu.SMEM),
            pl.BlockSpec(memory_space=pltpu.VMEM),
        ],
        out_specs=[pl.BlockSpec(memory_space=pltpu.VMEM)] * 2,
        out_shape=[
            jax.ShapeDtypeStruct((64, 24, 128), BF16),
            jax.ShapeDtypeStruct((8, 128), F32),
        ],
        compiler_params=pltpu.CompilerParams(vmem_limit_bytes=16 * 1024 * 1024),
        cost_estimate=pl.CostEstimate(
            flops=1_000_000, bytes_accessed=1_600_000, transcendentals=0
        ),
        name="combine",
    )(y_high, got)


def unpack_kernel(place_at, back, theirs, whole, head_weight, weights, mods):
    for source, half in ((back, place_at[0]), (theirs, 1 - place_at[0])):
        rows = source[...].astype(F32).reshape(64, 24 * 128)
        weights[:, pl.ds(pl.multiple_of(half * HALF, 128), HALF)] = rows[:, 0:HALF]
    summed = whole[:, 32:96]
    high = summed.astype(BF16)
    low = (summed - high.astype(F32)).astype(BF16)
    shifts = jnp.dot(high, head_weight[...], preferred_element_type=F32) + jnp.dot(
        low, head_weight[...], preferred_element_type=F32
    )
    for y_low in range(2):
        mods[y_low, 0:1, :] = shifts[y_low : y_low + 1]
    for part in range(20):
        rows = back[place_at[1] * 32 + part].astype(F32)
        for y_low in range(2):
            for near in range(2):
                at = (2 * part + near) * 128
                row = 20 + 2 * y_low + near
                mods[y_low, 1:2, at : at + 128] = rows[row : row + 1]


def unpack(place_at, back, theirs, whole, head_weight):
    return pl.pallas_call(
        unpack_kernel,
        in_specs=[pl.BlockSpec(memory_space=pltpu.SMEM)]
        + [pl.BlockSpec(memory_space=pltpu.VMEM)] * 4,
        out_specs=[pl.BlockSpec(memory_space=pltpu.VMEM)] * 2,
        out_shape=[
            jax.ShapeDtypeStruct((64, WIDTH), F32),
            jax.ShapeDtypeStruct((2, 2, WIDTH), F32),
        ],
        compiler_params=pltpu.CompilerParams(vmem_limit_bytes=24 * 1024 * 1024),
        cost_estimate=pl.CostEstimate(
            flops=10_000_000, bytes_accessed=3_000_000, transcendentals=0
        ),
        name="unpack",
    )(place_at, back, theirs, whole, head_weight)


def hidden_kernel(terms, states, head_weight, mods, stat, out):
    patch = terms[:, 256:320].astype(BF16)
    grad = jnp.dot(patch, head_weight[...], preferred_element_type=F32)
    inv_std = stat[:, 128:129]
    normed = (states[...].astype(F32) - stat[:, 0:1]) * inv_std
    scaled = grad * (1.0 + mods[1:2, :])
    out[...] = ((scaled - terms[:, 0:1] - normed * terms[:, 128:129]) * inv_std).astype(BF16)


def hidden_grads(terms, states, head_weight, mods, stat):
    tokens = states.shape[0]
    fixed = lambda *shape: pl.BlockSpec(shape, lambda i: (0, 0))
    return pl.pallas_call(
        hidden_kernel,
        grid=(WIDTH // STEP,),
        in_specs=[
            fixed(tokens, 384),
            pl.BlockSpec((tokens, STEP), lambda i: (0, i)),
            pl.BlockSpec((64, STEP), lambda i: (0, i)),
            pl.BlockSpec((2, STEP), lambda i: (0, i)),
            fixed(tokens, 256),
        ],
        out_specs=pl.BlockSpec((tokens, STEP), lambda i: (0, i)),
        out_shape=jax.ShapeDtypeStruct((tokens, WIDTH), BF16),
        compiler_params=pltpu.CompilerParams(vmem_limit_bytes=LARGE),
        cost_estimate=pl.CostEstimate(
            flops=2 * 192 * 128 * WIDTH, bytes_accessed=6_000_000, transcendentals=0
        ),
        name="hidden_grads",
    )(terms, states, head_weight, mods, stat)


def channel_order(core, x, z, y_low):
    at = jnp.arange(CH, dtype=jnp.int32)
    first, second, rel, inner = at // 96, (at // 24) % 4, (at // 12) % 2, at % 12
    x_at = (x + jnp.where(core == 0, second, first)) % 4
    z_at = (z + jnp.where(core == 0, first, second)) % 4
    channel = 12 * ((y_low ^ rel) * 16 + x_at * 4 + z_at) + inner
    return (channel[:, None] == jnp.arange(CH, dtype=jnp.int32)[None, :]).astype(BF16)


def sum_kernel(first, second, third, fourth, *outs):
    rows = outs[0].shape[1]
    for tap in range(first.shape[0]):
        total = (first[tap].astype(F32) + second[tap].astype(F32)) + (
            third[tap].astype(F32) + fourth[tap].astype(F32)
        )
        for part, out in enumerate(outs):
            out[tap] = total[part * rows : (part + 1) * rows].astype(BF16)


def sum_parts(terms, count):
    taps, rows, _ = terms[0].shape
    block = lambda height: pl.BlockSpec((taps // 2, height, CH), lambda i: (i, 0, 0))
    return pl.pallas_call(
        sum_kernel,
        grid=(2,),
        in_specs=[block(rows)] * 4,
        out_specs=[block(rows // count)] * count,
        out_shape=[jax.ShapeDtypeStruct((taps, rows // count, CH), BF16)] * count,
        compiler_params=pltpu.CompilerParams(vmem_limit_bytes=LARGE),
        cost_estimate=pl.CostEstimate(flops=1, bytes_accessed=1, transcendentals=0),
        name="sum_parts",
    )(*terms)


def last_kernel(same, far, upper, lower, out):
    out[...] = (same[...].astype(F32) + far[...].astype(F32)) + (
        upper[...].astype(F32) + lower[...].astype(F32)
    )


def last_sum(*terms):
    return pl.pallas_call(
        last_kernel,
        in_specs=[IN_VMEM] * 4,
        out_specs=IN_VMEM,
        out_shape=jax.ShapeDtypeStruct(terms[0].shape, F32),
        compiler_params=pltpu.CompilerParams(vmem_limit_bytes=8 * 1024 * 1024),
        cost_estimate=pl.CostEstimate(flops=1, bytes_accessed=1, transcendentals=0),
        name="last_sum",
    )(*terms)


def added(*terms):
    return functools.reduce(lambda a, b: a + b, [term.astype(F32) for term in terms])


def local(
    features, pixel_grad, frame_list, conv_weight, in_weight, last_hidden, modulation, head_weight
):
    clips, frames, rows_here, columns, _ = features.shape
    clip = lax.axis_index("clip")
    tile = lax.axis_index("tile")
    _, x, z, core = place(clip, tile)
    y_low = tile // 16

    up = [(i, i + 1) for i in range(31)]
    down = [(i + 1, i) for i in range(31)]
    border = [
        jnp.transpose(pixel_grad[:, :, row], (2, 0, 1, 3)).reshape(columns, SPAN, CH)
        for row in (0, 1)
    ]
    low = lax.ppermute(border[1], "tile", up)
    high = lax.ppermute(border[0], "tile", down)

    scored = jnp.any(
        frame_list[:, None, :] == jnp.arange(frames, dtype=jnp.int32)[None, :, None], axis=-1
    ).astype(BF16)
    keep = jnp.broadcast_to(scored.reshape(SPAN, 1), (SPAN, CH))
    masked = pixel_grad * scored[:, :, None, None, None]
    own = jnp.transpose(masked, (2, 3, 0, 1, 4)).reshape(rows_here, columns, SPAN, CH)
    feats = jnp.transpose(features, (2, 3, 0, 1, 4)).reshape(rows_here, columns, SPAN, CH)
    own2 = lax.ppermute(own, BOTH, OTHER_CORE)
    acts = jax.nn.silu(feats.astype(F32)).astype(BF16)
    acts2 = lax.ppermute(acts, BOTH, OTHER_CORE)
    keep2 = lax.ppermute(keep, BOTH, OTHER_CORE)
    low2 = lax.ppermute(low, BOTH, OTHER_CORE)
    high2 = lax.ppermute(high, BOTH, OTHER_CORE)

    mods = lax.dynamic_index_in_dim(modulation, y_low, 0, keepdims=False)
    head_t = head_weight.T
    core_at = core.astype(jnp.int32).reshape(1)
    y_high = (clip // 2).astype(jnp.int32).reshape(1)
    order = channel_order(core, x, z, y_low)
    parts = weight_grad(
        core_at, own, low, high, keep, acts, own2, low2, high2, keep2, acts2, order
    )
    moved = [lax.ppermute(parts[k], BOTH, along(0, k)) for k in (1, 2, 3)]

    low, high, _ = lax.optimization_barrier((low, high, parts))
    sent = input_grad(own, low, high, keep, feats, conv_weight, in_weight)
    states, _ = lax.optimization_barrier((last_hidden, sent))
    stat = stats(states)
    sent = lax.all_to_all(sent, "tile", 0, 0, tiled=True)
    moved, _ = lax.optimization_barrier((moved, stat))
    rows = sum_parts([parts[0], *moved], 4)
    sent, rows = lax.optimization_barrier((sent, rows))
    load, give, terms = head_sums(core_at, sent, last_hidden, head_t, mods, stat)
    taken = lax.ppermute(give, BOTH, OTHER_CORE)
    load = added(load, taken).astype(BF16)
    got = lax.all_to_all(load, BOTH, 0, 0, tiled=True, axis_index_groups=SAME_CORE)
    moved = [lax.ppermute(rows[k], BOTH, along(1, k)) for k in (1, 2, 3)]
    got, rows = lax.optimization_barrier((got, rows))

    back, whole_patch = combine(y_high, got)
    moved, _ = lax.optimization_barrier((moved, back))
    same, flipped = sum_parts([rows[0], *moved], 2)
    terms, same, flipped = lax.optimization_barrier((terms, same, flipped))
    hidden_grad = hidden_grads(terms, last_hidden, head_t, mods, stat)
    far = lax.ppermute(same, BOTH, along_y(2))
    upper = lax.ppermute(flipped, BOTH, along_y(1))
    lower = lax.ppermute(flipped, BOTH, along_y(3))
    back = lax.all_to_all(back, BOTH, 0, 0, tiled=True, axis_index_groups=SAME_CORE)
    share = last_sum(same, far, upper, lower)
    share, hidden_grad, _ = lax.optimization_barrier((share, hidden_grad, back))
    other = lax.ppermute(back, BOTH, OTHER_CORE)
    weights, modulation_grad = unpack(
        jnp.concatenate([core_at, y_high]), back, other, whole_patch, head_t
    )

    theirs = lax.ppermute(share, BOTH, OTHER_CORE)
    first = jnp.where(core == 0, share, theirs)
    second = jnp.where(core == 0, theirs, share)
    conv_weight_grad = jnp.concatenate([first, second[10:], second[:9]], axis=0)
    return (
        hidden_grad, weights.T, modulation_grad, conv_weight_grad.reshape(3, 3, 3, 12, CH)
    )


def solution(mesh):
    return jax.shard_map(
        local,
        mesh=mesh,
        in_specs=(
            P("clip", None, "tile", None, None),
            P("clip", None, "tile", None, None),
            P("clip", None),
            P(),
            P(),
            P(("clip", "tile"), None),
            P("clip", None, None),
            P(),
        ),
        out_specs=(
            P(("clip", "tile"), None),
            P(),
            P("clip", None, None),
            P(None, None, None, "tile", None),
        ),
        check_vma=False,
    )
```

```python
import functools

import jax
import jax.numpy as jnp
from jax import lax
from jax.experimental import pallas as pl
from jax.experimental.pallas import tpu as pltpu
from jax.sharding import PartitionSpec as P

F32 = jnp.float32
BF16 = jnp.bfloat16
BOTH = ("clip", "tile")
FRAMES = 16
SPAN = 32
COLS = 12
CH = 384
WIDTH = 5120
HALF = 2560
STEP = 1280
TAPS = 14
LARGE = 56 * 1024 * 1024
IN_VMEM = pl.BlockSpec(memory_space=pltpu.VMEM)


def place(clip, tile):
    return (clip // 2) * 2 + tile // 16, (tile // 4) % 4, tile % 4, clip % 2


def number(y, x, z, core):
    return ((y // 2) * 2 + core) * 32 + (y % 2) * 16 + x * 4 + z


def pairs(shift_of):
    out = []
    for source in range(128):
        where = place(source // 32, source % 32)
        out.append((source, number(*shift_of(*where))))
    return out


def along(core_axis, steps):
    def shift(y, x, z, core):
        if core == core_axis:
            return y, x, (z + steps) % 4, core
        return y, (x + steps) % 4, z, core

    return pairs(shift)


def along_y(steps):
    return pairs(lambda y, x, z, core: ((y + steps) % 4, x, z, core))


SAME_CORE = [[c * 32 + t for c in (core, core + 2) for t in range(32)] for core in (0, 1)]
OTHER_CORE = pairs(lambda y, x, z, core: (y, x, z, 1 - core))


def shift_frames(tile, steps):
    if steps == 0:
        return tile
    count = tile.shape[0]
    moved = pltpu.roll(tile, count - steps, 0)
    frame = lax.broadcasted_iota(jnp.int32, tile.shape, 0) & (FRAMES - 1)
    return jnp.where(frame < FRAMES - steps, moved, 0.0)


def fill_row(padded, source, base, keep=None):
    blank = jnp.zeros((SPAN, CH), BF16)
    padded[0, pl.ds(base, SPAN)] = blank
    padded[COLS + 1, pl.ds(base, SPAN)] = blank
    rows = source[...]
    padded[pl.ds(1, COLS), pl.ds(base, SPAN)] = rows if keep is None else rows * keep[...]


def lanes_dot(left, right):
    return lax.dot_general(left, right, (((1,), (1,)), ((), ())), preferred_element_type=F32)


def column_windows(rows):
    return jnp.concatenate(
        [rows[:, 2 - col_tap : 2 - col_tap + COLS].reshape(-1, CH) for col_tap in range(3)], axis=1
    )


def tap_weights(weight):
    return jnp.concatenate(
        [
            jnp.concatenate([weight[time_tap, 0, col_tap] for col_tap in range(3)], axis=1)
            for time_tap in range(3)
        ],
        axis=0,
    )


def grad_kernel(
    own, low, high, keep, feats, weight, in_weight, out, padded, total, grads, spread
):
    step = pl.program_id(0)

    @pl.when(step == 0)
    def _():
        for row, source in enumerate((low, own.at[0], own.at[1], high)):
            fill_row(padded.at[row], source, 0, None if row in (1, 2) else keep)
        total[...] = lanes_dot(column_windows(padded.at[1:3]), tap_weights(weight))
        blank = jnp.zeros((16, CH), BF16)
        for time_tap in range(3):
            for rowout in range(4):
                for parity in range(2):
                    at = ((time_tap * 4 + rowout) * 2 + parity) * 16
                    for near in range(4):
                        for side in range(2):
                            row_tap = rowout - side
                            col_tap = parity + 2 - near
                            inside = 0 <= row_tap <= 2 and 0 <= col_tap <= 2
                            value = in_weight[time_tap, row_tap, col_tap] if inside else blank
                            spread[at : at + 16, pl.ds((near * 2 + side) * CH, CH)] = value

    @pl.when(step == 1)
    def _():
        total[...] += lanes_dot(column_windows(padded.at[2:4]), tap_weights(weight))

    def finish(side, source):
        blank = jnp.zeros((SPAN, CH), BF16)
        grads[side, 0, 0] = blank
        grads[side, 6, 1] = blank
        for col in range(COLS):
            values = feats[side, col].astype(F32)
            sig = jax.nn.sigmoid(values)
            slope = sig * (1.0 + values * (1.0 - sig))
            tile = source[col * SPAN : (col + 1) * SPAN]
            summed = (
                tile[:, 0:CH]
                + shift_frames(tile[:, CH : 2 * CH], 1)
                + shift_frames(tile[:, 2 * CH : 3 * CH], 2)
            )
            grads[side, (col + 1) // 2, (col + 1) % 2] = (summed * slope).astype(BF16)

    @pl.when(step == 2)
    def _():
        total[...] += lanes_dot(column_windows(padded.at[0:2]), tap_weights(weight))
        for side in range(2):
            finish(side, total.at[side * 384 : (side + 1) * 384])
        left = jnp.concatenate(
            [
                grads[side, pl.ds(near // 2, 6), near % 2].reshape(-1, CH)
                for near in range(4)
                for side in range(2)
            ],
            axis=1,
        )
        latent = lanes_dot(left, spread[...])
        for pair in range(6):
            block = latent[pair * SPAN : (pair + 1) * SPAN]
            out[:, pair, :] = (
                block[:, 0:128]
                + shift_frames(block[:, 128:256], 1)
                + shift_frames(block[:, 256:384], 2)
            )
        out[:, 6:8, :] = jnp.zeros((SPAN, 2, 128), F32)


def whole(*shape):
    return pl.BlockSpec(shape, lambda i: (0,) * len(shape))


def input_grad(own, low, high, keep, feats, conv_weight, in_weight):
    return pl.pallas_call(
        grad_kernel,
        grid=(3,),
        in_specs=[
            whole(2, COLS, SPAN, CH),
            whole(COLS, SPAN, CH),
            whole(COLS, SPAN, CH),
            whole(SPAN, CH),
            whole(2, COLS, SPAN, CH),
            pl.BlockSpec((3, 1, 3, CH, CH), lambda i: (0, jnp.where(i == 2, 2, 1 - i), 0, 0, 0)),
            whole(3, 3, 3, 16, CH),
        ],
        out_specs=whole(SPAN, 8, 128),
        out_shape=jax.ShapeDtypeStruct((SPAN, 8, 128), F32),
        scratch_shapes=[
            pltpu.VMEM((4, COLS + 2, SPAN, CH), BF16),
            pltpu.VMEM((2 * COLS * SPAN, 3 * CH), F32),
            pltpu.VMEM((2, 7, 2, SPAN, CH), BF16),
            pltpu.VMEM((384, 8 * CH), BF16),
        ],
        compiler_params=pltpu.CompilerParams(vmem_limit_bytes=LARGE),
        cost_estimate=pl.CostEstimate(
            flops=2 * 768 * 27 * CH * CH, bytes_accessed=12_000_000, transcendentals=768 * CH
        ),
        name="input_grad",
    )(own, low, high, keep, feats, conv_weight, in_weight)


def weight_kernel(
    core, own, low, high, keep, acts, own2, low2, high2, keep2, acts2, order,
    out0, out1, out2, out3, padded, active, turned,
):
    step = pl.program_id(0)

    @pl.when(step == 0)
    def _():
        for base, rows, kept in ((0, (low, own.at[0], own.at[1], high), keep),
                                 (SPAN, (low2, own2.at[0], own2.at[1], high2), keep2)):
            for row, source in enumerate(rows):
                fill_row(padded.at[row], source, base, None if row in (1, 2) else kept)
        for base, source in ((0, acts), (SPAN, acts2)):
            active[:, :, pl.ds(base, SPAN)] = source[...]
        frame = lax.broadcasted_iota(jnp.int32, (CH, 128), 1) & (FRAMES - 1)
        across = lanes_dot(order[...], active[...].reshape(-1, CH))
        for at in range(0, 2 * COLS * 2 * SPAN, 128):
            values = across[:, at : at + 128]
            one = jnp.where(frame >= 1, pltpu.roll(values, 1, 1), 0.0)
            two = jnp.where(frame >= 2, pltpu.roll(values, 2, 1), 0.0)
            turned[0, :, at : at + 128] = jnp.where(core[0] == 0, values, two).astype(BF16)
            turned[1, :, at : at + 128] = one.astype(BF16)

    def window(place_at):
        tap = jnp.where(place_at < 9, place_at, place_at - 9 + 4 * core[0])
        row_tap = lax.div(tap, 3)
        col_tap = tap - 3 * row_tap
        return padded[pl.ds(2 - row_tap, 2), pl.ds(2 - col_tap, COLS)].reshape(-1, CH)

    def write(which, product):
        for part, out in enumerate((out0, out1, out2, out3)):
            out[which] = product[part * 96 : (part + 1) * 96].astype(BF16)

    @pl.when(step != 4)
    def _():
        right = jnp.concatenate([window(2 * step), window(2 * step + 1)], axis=1)
        slot = jnp.where(step < 4, 0, 1)
        product = jnp.dot(turned[slot], right, preferred_element_type=F32)
        write(0, product[:, 0:CH])
        write(1, product[:, CH : 2 * CH])

    @pl.when(step == 4)
    def _():
        for slot in range(2):
            write(slot, jnp.dot(turned[slot], window(8 + slot), preferred_element_type=F32))


def weight_grad(core, own, low, high, keep, acts, own2, low2, high2, keep2, acts2, order):
    rows = [whole(2, COLS, SPAN, CH), whole(COLS, SPAN, CH), whole(COLS, SPAN, CH),
            whole(SPAN, CH), whole(2, COLS, SPAN, CH)]
    return pl.pallas_call(
        weight_kernel,
        grid=(TAPS // 2,),
        in_specs=[pl.BlockSpec(memory_space=pltpu.SMEM), *rows, *rows, whole(CH, CH)],
        out_specs=[pl.BlockSpec((2, 96, CH), lambda i: (i, 0, 0))] * 4,
        out_shape=[jax.ShapeDtypeStruct((TAPS, 96, CH), BF16)] * 4,
        scratch_shapes=[
            pltpu.VMEM((4, COLS + 2, 2 * SPAN, CH), BF16),
            pltpu.VMEM((2, COLS, 2 * SPAN, CH), BF16),
            pltpu.VMEM((2, CH, 2 * COLS * 2 * SPAN), BF16),
        ],
        compiler_params=pltpu.CompilerParams(vmem_limit_bytes=LARGE),
        cost_estimate=pl.CostEstimate(
            flops=2 * 1536 * TAPS * CH * CH, bytes_accessed=12_000_000, transcendentals=1536 * CH
        ),
        name="weight_grad",
    )(core, own, low, high, keep, acts, own2, low2, high2, keep2, acts2, order)


def stats_kernel(states, stat):
    blocks = [slice(at, at + 128) for at in range(0, WIDTH, 128)]
    summed = jnp.zeros((32, 128), F32)
    for block in blocks:
        summed = summed + states[:, block].astype(F32)
    average = jnp.sum(summed, axis=-1, keepdims=True) * (1.0 / WIDTH)
    spread = jnp.broadcast_to(average, (32, 128))
    summed = jnp.zeros((32, 128), F32)
    for block in blocks:
        centered = states[:, block].astype(F32) - spread
        summed = summed + centered * centered
    variance = jnp.sum(summed, axis=-1, keepdims=True) * (1.0 / WIDTH)
    inv_std = jnp.broadcast_to(lax.rsqrt(variance + 1e-06), (32, 128))
    stat[:, 0:128] = spread
    stat[:, 128:256] = inv_std


def stats(states):
    tokens = states.shape[0]
    return pl.pallas_call(
        stats_kernel,
        grid=(tokens // 32,),
        in_specs=[pl.BlockSpec((32, WIDTH), lambda i: (i, 0))],
        out_specs=pl.BlockSpec((32, 256), lambda i: (i, 0)),
        out_shape=jax.ShapeDtypeStruct((tokens, 256), F32),
        compiler_params=pltpu.CompilerParams(vmem_limit_bytes=8 * 1024 * 1024),
        cost_estimate=pl.CostEstimate(flops=1, bytes_accessed=1, transcendentals=0),
        name="token_stats",
    )(states)


def head_kernel(
    core, sent, states, head_weight, mods, stat,
    load, give, terms, patch, patch_t, total, gains, whole, piece, sums, dots,
):
    step = pl.program_id(0)
    tokens = patch.shape[0]

    @pl.when(step == 0)
    def _():
        below = lax.broadcasted_iota(jnp.int32, (SPAN, 128), 0)
        lane = lax.broadcasted_iota(jnp.int32, (SPAN, 128), 1)
        parts = []
        for pair in range(6):
            here = sent[:, pair, :]
            swapped = pltpu.roll(here, 64, 1)
            before = jnp.where(below > 0, pltpu.roll(swapped, 1, 0), 0.0)
            after = jnp.where(below < SPAN - 1, pltpu.roll(swapped, SPAN - 1, 0), 0.0)
            summed = here + jnp.where(lane < 64, before, after)
            inside = (lane >= 32) & (lane < 96)
            parts.append(jnp.where(inside, summed, 0.0).astype(BF16))
        stacked = jnp.concatenate(parts, axis=0)
        token = lax.broadcasted_iota(jnp.int32, (tokens, tokens), 0)
        source = lax.broadcasted_iota(jnp.int32, (tokens, tokens), 1)
        match = (source & (SPAN - 1)) * 6 + lax.shift_right_logical(source, 5) == token
        pick = jnp.where(match, 1.0, 0.0).astype(BF16)
        ordered = jnp.dot(pick, stacked, preferred_element_type=F32)
        patch[...] = ordered[:, 32:96].astype(BF16)
        terms[:, 256:384] = jnp.concatenate([ordered[:, 32:96], ordered[:, 32:96]], axis=1)
        patch_t[...] = ordered.T[32:96].astype(BF16)
        whole[...] = jnp.broadcast_to(jnp.sum(ordered, axis=0, keepdims=True), whole.shape)
        sums[...] = jnp.zeros_like(sums)
        dots[...] = jnp.zeros_like(dots)
        piece[...] = jnp.zeros_like(piece)

    grad = jnp.dot(patch[...], head_weight[...], preferred_element_type=F32)
    normed = (states[...].astype(F32) - stat[:, 0:1]) * stat[:, 128:129]
    weighted = grad * normed
    at = pl.multiple_of(step * STEP, STEP)
    gains[0:1, pl.ds(at, STEP)] = jnp.sum(weighted, axis=0, keepdims=True)
    scale = 1.0 + mods[1:2, :]
    sums[...] += jnp.sum(grad * scale, axis=-1, keepdims=True)
    dots[...] += jnp.sum(weighted * scale, axis=-1, keepdims=True)
    head_input = (normed * scale + mods[0:1, :]).astype(BF16)
    total[:, pl.ds(at, STEP)] = jnp.dot(patch_t[...], head_input, preferred_element_type=F32)

    @pl.when(step == pl.num_programs(0) - 1)
    def _():
        for block in range(40):
            piece[block // 2 : block // 2 + 1, pl.ds((block % 2) * 128, 128)] = gains[
                0:1, block * 128 : (block + 1) * 128
            ]
        extra = jnp.concatenate([piece[...], whole[...], jnp.zeros((32, 128), F32)], axis=1)
        extra = jnp.concatenate([extra, extra], axis=0)
        for out, half in ((load, core[0]), (give, 1 - core[0])):
            rows = total[:, pl.ds(pl.multiple_of(half * HALF, 128), HALF)]
            rows = jnp.concatenate([rows, extra if out is load else extra * 0.0], axis=1)
            out[...] = rows.reshape(64, 24, 128).astype(BF16)
        terms[:, 0:128] = sums[...] * (1.0 / WIDTH)
        terms[:, 128:256] = dots[...] * (1.0 / WIDTH)


def head_sums(core, sent, states, head_weight, mods, stat):
    tokens = states.shape[0]
    fixed = lambda *shape: pl.BlockSpec(shape, lambda i: (0,) * len(shape))
    return pl.pallas_call(
        head_kernel,
        grid=(WIDTH // STEP,),
        in_specs=[
            pl.BlockSpec(memory_space=pltpu.SMEM),
            fixed(SPAN, 8, 128),
            pl.BlockSpec((tokens, STEP), lambda i: (0, i)),
            pl.BlockSpec((64, STEP), lambda i: (0, i)),
            pl.BlockSpec((2, STEP), lambda i: (0, i)),
            fixed(tokens, 256),
        ],
        out_specs=[fixed(64, 24, 128), fixed(64, 24, 128), fixed(tokens, 384)],
        out_shape=[
            jax.ShapeDtypeStruct((64, 24, 128), BF16),
            jax.ShapeDtypeStruct((64, 24, 128), BF16),
            jax.ShapeDtypeStruct((tokens, 384), F32),
        ],
        scratch_shapes=[
            pltpu.VMEM((tokens, 64), BF16),
            pltpu.VMEM((64, tokens), BF16),
            pltpu.VMEM((64, WIDTH), F32),
            pltpu.VMEM((1, WIDTH), F32),
            pltpu.VMEM((32, 128), F32),
            pltpu.VMEM((32, 256), F32),
            pltpu.VMEM((tokens, 128), F32),
            pltpu.VMEM((tokens, 128), F32),
        ],
        compiler_params=pltpu.CompilerParams(vmem_limit_bytes=32 * 1024 * 1024),
        cost_estimate=pl.CostEstimate(
            flops=2 * 2 * 192 * 128 * WIDTH, bytes_accessed=7_000_000, transcendentals=0
        ),
        name="head_sums",
    )(core, sent, states, head_weight, mods, stat)


def combine_kernel(y_high, got, back, whole):
    def add(at, carry):
        for near in range(8):
            carry = carry + got[at * 8 + near].astype(F32)
        return carry

    total = lax.fori_loop(0, 8, add, jnp.zeros((24, 128), F32))
    mine = []
    for y_low in range(2):
        summed = jnp.zeros((24, 128), F32)
        for near in range(16):
            summed = summed + got[y_high[0] * 32 + y_low * 16 + near].astype(F32)
        mine.append(summed)
    row = lax.broadcasted_iota(jnp.int32, (24, 128), 0)
    line = jnp.where(row < 20, total, jnp.where(row < 22, mine[0], pltpu.roll(mine[1], 2, 0)))
    back[...] = jnp.broadcast_to(line.astype(BF16)[None], back.shape)
    whole[...] = jnp.zeros_like(whole)
    whole[0:1] = mine[0][22:23]
    whole[1:2] = mine[1][22:23]


def combine(y_high, got):
    return pl.pallas_call(
        combine_kernel,
        in_specs=[
            pl.BlockSpec(memory_space=pltpu.SMEM),
            pl.BlockSpec(memory_space=pltpu.VMEM),
        ],
        out_specs=[pl.BlockSpec(memory_space=pltpu.VMEM)] * 2,
        out_shape=[
            jax.ShapeDtypeStruct((64, 24, 128), BF16),
            jax.ShapeDtypeStruct((8, 128), F32),
        ],
        compiler_params=pltpu.CompilerParams(vmem_limit_bytes=16 * 1024 * 1024),
        cost_estimate=pl.CostEstimate(
            flops=1_000_000, bytes_accessed=1_600_000, transcendentals=0
        ),
        name="combine",
    )(y_high, got)


def unpack_kernel(place_at, back, theirs, whole, head_weight, weights, mods):
    for source, half in ((back, place_at[0]), (theirs, 1 - place_at[0])):
        rows = source[...].astype(F32).reshape(64, 24 * 128)
        weights[:, pl.ds(pl.multiple_of(half * HALF, 128), HALF)] = rows[:, 0:HALF]
    summed = whole[:, 32:96]
    high = summed.astype(BF16)
    low = (summed - high.astype(F32)).astype(BF16)
    shifts = jnp.dot(high, head_weight[...], preferred_element_type=F32) + jnp.dot(
        low, head_weight[...], preferred_element_type=F32
    )
    for y_low in range(2):
        mods[y_low, 0:1, :] = shifts[y_low : y_low + 1]
    for part in range(20):
        rows = back[place_at[1] * 32 + part].astype(F32)
        for y_low in range(2):
            for near in range(2):
                at = (2 * part + near) * 128
                row = 20 + 2 * y_low + near
                mods[y_low, 1:2, at : at + 128] = rows[row : row + 1]


def unpack(place_at, back, theirs, whole, head_weight):
    return pl.pallas_call(
        unpack_kernel,
        in_specs=[pl.BlockSpec(memory_space=pltpu.SMEM)]
        + [pl.BlockSpec(memory_space=pltpu.VMEM)] * 4,
        out_specs=[pl.BlockSpec(memory_space=pltpu.VMEM)] * 2,
        out_shape=[
            jax.ShapeDtypeStruct((64, WIDTH), F32),
            jax.ShapeDtypeStruct((2, 2, WIDTH), F32),
        ],
        compiler_params=pltpu.CompilerParams(vmem_limit_bytes=24 * 1024 * 1024),
        cost_estimate=pl.CostEstimate(
            flops=10_000_000, bytes_accessed=3_000_000, transcendentals=0
        ),
        name="unpack",
    )(place_at, back, theirs, whole, head_weight)


def hidden_kernel(terms, states, head_weight, mods, stat, out):
    patch = terms[:, 256:320].astype(BF16)
    grad = jnp.dot(patch, head_weight[...], preferred_element_type=F32)
    inv_std = stat[:, 128:129]
    normed = (states[...].astype(F32) - stat[:, 0:1]) * inv_std
    scaled = grad * (1.0 + mods[1:2, :])
    out[...] = ((scaled - terms[:, 0:1] - normed * terms[:, 128:129]) * inv_std).astype(BF16)


def hidden_grads(terms, states, head_weight, mods, stat):
    tokens = states.shape[0]
    fixed = lambda *shape: pl.BlockSpec(shape, lambda i: (0, 0))
    return pl.pallas_call(
        hidden_kernel,
        grid=(WIDTH // STEP,),
        in_specs=[
            fixed(tokens, 384),
            pl.BlockSpec((tokens, STEP), lambda i: (0, i)),
            pl.BlockSpec((64, STEP), lambda i: (0, i)),
            pl.BlockSpec((2, STEP), lambda i: (0, i)),
            fixed(tokens, 256),
        ],
        out_specs=pl.BlockSpec((tokens, STEP), lambda i: (0, i)),
        out_shape=jax.ShapeDtypeStruct((tokens, WIDTH), BF16),
        compiler_params=pltpu.CompilerParams(vmem_limit_bytes=LARGE),
        cost_estimate=pl.CostEstimate(
            flops=2 * 192 * 128 * WIDTH, bytes_accessed=6_000_000, transcendentals=0
        ),
        name="hidden_grads",
    )(terms, states, head_weight, mods, stat)


def channel_order(core, x, z, y_low):
    at = jnp.arange(CH, dtype=jnp.int32)
    first, second, rel, inner = at // 96, (at // 24) % 4, (at // 12) % 2, at % 12
    x_at = (x + jnp.where(core == 0, second, first)) % 4
    z_at = (z + jnp.where(core == 0, first, second)) % 4
    channel = 12 * ((y_low ^ rel) * 16 + x_at * 4 + z_at) + inner
    return (channel[:, None] == jnp.arange(CH, dtype=jnp.int32)[None, :]).astype(BF16)


def sum_kernel(first, second, third, fourth, *outs):
    rows = outs[0].shape[1]
    for tap in range(first.shape[0]):
        total = (first[tap].astype(F32) + second[tap].astype(F32)) + (
            third[tap].astype(F32) + fourth[tap].astype(F32)
        )
        for part, out in enumerate(outs):
            out[tap] = total[part * rows : (part + 1) * rows].astype(BF16)


def sum_parts(terms, count):
    taps, rows, _ = terms[0].shape
    block = lambda height: pl.BlockSpec((taps // 2, height, CH), lambda i: (i, 0, 0))
    return pl.pallas_call(
        sum_kernel,
        grid=(2,),
        in_specs=[block(rows)] * 4,
        out_specs=[block(rows // count)] * count,
        out_shape=[jax.ShapeDtypeStruct((taps, rows // count, CH), BF16)] * count,
        compiler_params=pltpu.CompilerParams(vmem_limit_bytes=LARGE if count == 4 else 16 * 1024 * 1024),
        cost_estimate=pl.CostEstimate(flops=1, bytes_accessed=1, transcendentals=0),
        name="sum_parts",
    )(*terms)


def last_kernel(same, far, upper, lower, out):
    out[...] = (same[...].astype(F32) + far[...].astype(F32)) + (
        upper[...].astype(F32) + lower[...].astype(F32)
    )


def last_sum(*terms):
    return pl.pallas_call(
        last_kernel,
        in_specs=[IN_VMEM] * 4,
        out_specs=IN_VMEM,
        out_shape=jax.ShapeDtypeStruct(terms[0].shape, F32),
        compiler_params=pltpu.CompilerParams(vmem_limit_bytes=8 * 1024 * 1024),
        cost_estimate=pl.CostEstimate(flops=1, bytes_accessed=1, transcendentals=0),
        name="last_sum",
    )(*terms)


def added(*terms):
    return functools.reduce(lambda a, b: a + b, [term.astype(F32) for term in terms])


def local(
    features, pixel_grad, frame_list, conv_weight, in_weight, last_hidden, modulation, head_weight
):
    clips, frames, rows_here, columns, _ = features.shape
    clip = lax.axis_index("clip")
    tile = lax.axis_index("tile")
    _, x, z, core = place(clip, tile)
    y_low = tile // 16

    up = [(i, i + 1) for i in range(31)]
    down = [(i + 1, i) for i in range(31)]
    border = [
        jnp.transpose(pixel_grad[:, :, row], (2, 0, 1, 3)).reshape(columns, SPAN, CH)
        for row in (0, 1)
    ]
    low = lax.ppermute(border[1], "tile", up)
    high = lax.ppermute(border[0], "tile", down)

    scored = jnp.any(
        frame_list[:, None, :] == jnp.arange(frames, dtype=jnp.int32)[None, :, None], axis=-1
    ).astype(BF16)
    keep = jnp.broadcast_to(scored.reshape(SPAN, 1), (SPAN, CH))
    masked = pixel_grad * scored[:, :, None, None, None]
    own = jnp.transpose(masked, (2, 3, 0, 1, 4)).reshape(rows_here, columns, SPAN, CH)
    feats = jnp.transpose(features, (2, 3, 0, 1, 4)).reshape(rows_here, columns, SPAN, CH)
    own2 = lax.ppermute(own, BOTH, OTHER_CORE)
    acts = jax.nn.silu(feats.astype(F32)).astype(BF16)
    acts2 = lax.ppermute(acts, BOTH, OTHER_CORE)
    keep2 = lax.ppermute(keep, BOTH, OTHER_CORE)
    low2 = lax.ppermute(low, BOTH, OTHER_CORE)
    high2 = lax.ppermute(high, BOTH, OTHER_CORE)

    mods = lax.dynamic_index_in_dim(modulation, y_low, 0, keepdims=False)
    head_t = head_weight.T
    core_at = core.astype(jnp.int32).reshape(1)
    y_high = (clip // 2).astype(jnp.int32).reshape(1)
    order = channel_order(core, x, z, y_low)
    parts = weight_grad(
        core_at, own, low, high, keep, acts, own2, low2, high2, keep2, acts2, order
    )
    moved = [lax.ppermute(parts[k], BOTH, along(0, k)) for k in (1, 2, 3)]

    low, high, _ = lax.optimization_barrier((low, high, parts))
    sent = input_grad(own, low, high, keep, feats, conv_weight, in_weight)
    states, _ = lax.optimization_barrier((last_hidden, sent))
    stat = stats(states)
    sent = lax.all_to_all(sent, "tile", 0, 0, tiled=True)
    moved, _ = lax.optimization_barrier((moved, stat))
    rows = sum_parts([parts[0], *moved], 4)
    sent, rows = lax.optimization_barrier((sent, rows))
    load, give, terms = head_sums(core_at, sent, last_hidden, head_t, mods, stat)
    taken = lax.ppermute(give, BOTH, OTHER_CORE)
    load = added(load, taken).astype(BF16)
    got = lax.all_to_all(load, BOTH, 0, 0, tiled=True, axis_index_groups=SAME_CORE)
    moved = [lax.ppermute(rows[k], BOTH, along(1, k)) for k in (1, 2, 3)]
    got, rows = lax.optimization_barrier((got, rows))

    back, whole_patch = combine(y_high, got)
    moved, _ = lax.optimization_barrier((moved, back))
    same, flipped = sum_parts([rows[0], *moved], 2)
    terms, same, flipped = lax.optimization_barrier((terms, same, flipped))
    hidden_grad = hidden_grads(terms, last_hidden, head_t, mods, stat)
    far = lax.ppermute(same, BOTH, along_y(2))
    upper = lax.ppermute(flipped, BOTH, along_y(1))
    lower = lax.ppermute(flipped, BOTH, along_y(3))
    back = lax.all_to_all(back, BOTH, 0, 0, tiled=True, axis_index_groups=SAME_CORE)
    share = last_sum(same, far, upper, lower)
    share, hidden_grad, _ = lax.optimization_barrier((share, hidden_grad, back))
    other = lax.ppermute(back, BOTH, OTHER_CORE)
    weights, modulation_grad = unpack(
        jnp.concatenate([core_at, y_high]), back, other, whole_patch, head_t
    )

    theirs = lax.ppermute(share, BOTH, OTHER_CORE)
    first = jnp.where(core == 0, share, theirs)
    second = jnp.where(core == 0, theirs, share)
    conv_weight_grad = jnp.concatenate([first, second[10:], second[:9]], axis=0)
    return (
        hidden_grad, weights.T, modulation_grad, conv_weight_grad.reshape(3, 3, 3, 12, CH)
    )


def solution(mesh):
    return jax.shard_map(
        local,
        mesh=mesh,
        in_specs=(
            P("clip", None, "tile", None, None),
            P("clip", None, "tile", None, None),
            P("clip", None),
            P(),
            P(),
            P(("clip", "tile"), None),
            P("clip", None, None),
            P(),
        ),
        out_specs=(
            P(("clip", "tile"), None),
            P(),
            P("clip", None, None),
            P(None, None, None, "tile", None),
        ),
        check_vma=False,
    )
```
